512 devices in a mesh: section: 2 (over z_hi), seq: 32 (over y, z_lo), grp: 8 (over x, core).
Axes of the slice: x: 4, y: 8, z: 8 (z_hi: 2, z_lo: 4; z = z_hi * 4 + z_lo), core: 2. Of those that a mesh axis runs over, the one named last changes fastest.
Arguments:
- rows: bfloat16 [2, 8192, 3072], P('section', 'seq', 'grp'), may hold values from -1.5 to 1.5
- queries: bfloat16 [2, 8192, 2048], P('section', 'seq', 'grp'), may hold values from -6 to 6
- keys: bfloat16 [2, 8192, 2048], P('section', 'seq', 'grp'), may hold values from -6 to 6
- values: bfloat16 [2, 8192, 2048], P('section', 'seq', 'grp'), may hold values from -6 to 6
- text_kv: bfloat16 [2, 2, 256, 2048], P('section', None, 'grp'), may hold values from -6 to 6
- text_count: int32 [2], P('section'), may hold values from 32 to 256
- out_weight: bfloat16 [2, 2048, 3072], P('section', 'grp'), may hold values from -0.1875 to 0.1875
- gate: float32 [2, 3072], P('section', 'grp'), may hold values from 1 to 8
- band: int32 [64, 2], replicated, may hold values from 0 to 63, as said below
- tile_order: int32 [64], replicated, may hold values from 0 to 63, as said below
Outputs:
- handed: bfloat16 [2, 8192, 3072], P('section', 'seq', 'grp')
The draws below stay inside these ranges and needn't reach their ends.
Inputs may be any that keep to these rules, and one draw needn't show every extreme that they name: band[t, 0] <= t <= band[t, 1], and each side reaches at most 8 tiles from t; some tile reaches exactly 8 below itself. `tile_order`: a permutation of the tiles that moves each tile only within its aligned block of 4 stored positions.
All inputs are finite; a program needn't handle non-finite values.
Results may differ from the reference program's by a relative error of at most 0.0058.
Values may be sent and summed in bfloat16 or wider, within the bound.
No kernel may reach another device: no remote copies, remote signals or barrier semaphores. Data moves between devices by JAX's collectives and lax.ppermute only.
A program may use at most 64 MiB of HBM per device.

```python
import math
import jax
import jax.numpy as jnp
from jax import lax

D = 3072
HEADS = 16
HD = 128
TEXT = 256
TILE = 128
TOK_DEV = 256
SECTIONS = 2
TOKENS = 8192
TILES = 64
BAND_W = 8


def draw_band(key, part):
    key = jax.random.fold_in(key, 11)
    below_key, above_key = jax.random.split(key)
    tile_index = jnp.arange(TILES, dtype=jnp.int32)
    below = jax.random.randint(below_key, (TILES,), 0, BAND_W + 1)
    above = jax.random.randint(above_key, (TILES,), 0, BAND_W + 1)
    below = below.at[TILES // 2].set(BAND_W)
    low_end = jnp.maximum(tile_index - below, 0)
    high_end = jnp.minimum(tile_index + above, TILES - 1)
    return jnp.stack([low_end, high_end], axis=1).astype(jnp.int32)


def draw_tile_order(key, part):
    key = jax.random.fold_in(key, 23)
    block_len = 2 * (TOK_DEV // TILE)
    block_total = TILES // block_len
    scores = jax.random.randint(key, (block_total, block_len), 0, 1048576).astype(jnp.int32)
    scores = scores * block_len + jnp.arange(block_len, dtype=jnp.int32)[None, :]
    within = jnp.argsort(scores, axis=1).astype(jnp.int32)
    offsets = (jnp.arange(block_total, dtype=jnp.int32) * block_len)[:, None]
    return (within + offsets).reshape(TILES).astype(jnp.int32)


def spiked(result, stream_key, source, target, blocks, factor):
    def block_of(dim):
        return (jnp.arange(result.shape[dim]) // (result.shape[dim] // blocks)).reshape((-1,) + (1,) * (result.ndim - 1 - dim))

    near = jax.random.permutation(stream_key, blocks)[block_of(target)]
    other_side = (block_of(target) + blocks // 2) % blocks
    return jnp.where((block_of(source) == near) | (block_of(source) == other_side), factor * result, result)


def level_of(own_key, dims, shards, smallest, largest):
    factor_of, own = 1.0, jax.random.fold_in(own_key, 6)
    for axis_at, blocks in shards:
        draws = jnp.exp(jax.random.uniform(jax.random.fold_in(own, axis_at), (blocks,), jnp.float32, smallest / len(shards), largest / len(shards)))
        factor_of = factor_of * jnp.repeat(draws, dims[axis_at] // blocks).reshape([-1 if axis == axis_at else 1 for axis in range(len(dims))])
    return factor_of


def normal_values(stream_key, extent, spread, limit, cuts=(), kind=jnp.bfloat16):
    loudness = level_of(stream_key, extent, cuts, -0.22, 0.18) if cuts else 1.0
    result = jax.random.normal(stream_key, extent, jnp.float32) * spread * loudness
    return jnp.minimum(jnp.maximum(result, -limit), limit).astype(kind)


def noise_with(rng, shape, spread, limit, shards, heavy, kind=jnp.bfloat16):
    array = spread * jax.random.normal(rng, shape, jnp.float32)
    if shards:
        array = array * level_of(rng, shape, shards, -0.22, 0.18)
    return jnp.clip(spiked(array, jax.random.fold_in(rng, 3), *heavy), -limit, limit).astype(kind)


def setup_inputs(seed: int = 0) -> dict:
    key_list = jax.random.split(jax.random.key(seed), 11)
    rows = normal_values(key_list[0], (SECTIONS, TOKENS, D), 0.25, 1.5, ((0, 2), (1, 32), (2, 8)))
    queries = normal_values(key_list[1], (SECTIONS, TOKENS, HEADS * HD), 1.0, 6.0, ((0, 2), (1, 32), (2, 8)))
    keys = normal_values(key_list[2], (SECTIONS, TOKENS, HEADS * HD), 1.0, 6.0, ((0, 2), (1, 32), (2, 8)))
    values = normal_values(key_list[3], (SECTIONS, TOKENS, HEADS * HD), 1.0, 6.0, ((0, 2), (1, 32), (2, 8)))
    text_kv = normal_values(key_list[4], (SECTIONS, 2, TEXT, HEADS * HD), 1.0, 6.0, ((0, 2), (2, 8)))
    text_count = jax.random.randint(key_list[5], (SECTIONS,), TEXT // 8, TEXT + 1).astype(jnp.int32)
    out_weight = noise_with(key_list[6], (SECTIONS, HEADS * HD, D), (HEADS * HD) ** -0.5, 0.1875, ((0, 2), (1, 8)), (1, 2, 8, 2.0))
    gate = jnp.clip(jnp.exp(math.log(8.0) - 2.0794415 * jax.random.uniform(key_list[7], (SECTIONS, D), jnp.float32) ** level_of(key_list[7], (SECTIONS, D), ((0, 2), (1, 8)), -0.2, 0.2)), 1.0, 8.0)
    band = draw_band(jax.random.fold_in(key_list[10], 71), 0)
    tile_order = draw_tile_order(jax.random.fold_in(key_list[10], 71), 0)
    return {"rows": rows, "queries": queries, "keys": keys, "values": values, "text_kv": text_kv, "text_count": text_count, "out_weight": out_weight, "gate": gate, "band": band, "tile_order": tile_order}


def unit_norm(values_in, head_count):
    shaped = values_in.astype(jnp.float32).reshape(values_in.shape[:-1] + (head_count, HD))
    normed = shaped * lax.rsqrt(lax.optimization_barrier(jnp.mean(shaped * shaped, axis=-1, keepdims=True)) + 1e-06)
    return normed.reshape(values_in.shape).astype(jnp.bfloat16)

def one_block(rows, queries, keys, values, text_kv, text_count, out_weight, gate, band, tile_order):
    score_scale = HD ** (-0.5)
    query_n = unit_norm(queries, HEADS).reshape(TOKENS, HEADS, HD)
    key_n = unit_norm(keys, HEADS).reshape(TOKENS, HEADS, HD).astype(jnp.float32)
    value_h = values.reshape(TOKENS, HEADS, HD).astype(jnp.float32)
    text_key = unit_norm(text_kv[0], HEADS).reshape(TEXT, HEADS, HD).astype(jnp.float32)
    text_value = text_kv[1].reshape(TEXT, HEADS, HD).astype(jnp.float32)
    key_tile = tile_order[jnp.arange(TOKENS, dtype=jnp.int32) // TILE]
    text_live = jnp.arange(TEXT, dtype=jnp.int32) < text_count

    def one_tile(tile_pos):
        query_block = lax.dynamic_slice_in_dim(query_n, tile_pos * TILE, TILE, 0).astype(jnp.float32)
        query_tile = tile_order[tile_pos]
        allowed = (key_tile >= band[query_tile, 0]) & (key_tile <= band[query_tile, 1])
        scores = jnp.einsum('qhd,khd->hqk', query_block, key_n) * score_scale
        exp_video = jnp.where(allowed[None, None, :], jnp.exp(scores), 0.0)
        text_scores = jnp.einsum('qhd,khd->hqk', query_block, text_key) * score_scale
        exp_text = jnp.where(text_live[None, None, :], jnp.exp(text_scores), 0.0)
        denominator = lax.optimization_barrier(jnp.sum(exp_video, axis=-1)) + lax.optimization_barrier(jnp.sum(exp_text, axis=-1))
        numerator = jnp.einsum('hqk,khd->qhd', exp_video.astype(jnp.bfloat16).astype(jnp.float32), value_h)
        numerator = numerator + jnp.einsum('hqk,khd->qhd', exp_text.astype(jnp.bfloat16).astype(jnp.float32), text_value)
        return (numerator / denominator.T[:, :, None]).astype(jnp.bfloat16).reshape(TILE, HEADS * HD)
    attention = lax.map(one_tile, jnp.arange(TILES, dtype=jnp.int32)).reshape(TOKENS, HEADS * HD)
    projected = jnp.dot(attention, out_weight, preferred_element_type=jnp.float32)
    return (rows.astype(jnp.float32) + gate[None, :] * projected).astype(jnp.bfloat16)

def reference(rows, queries, keys, values, text_kv, text_count, out_weight, gate, band, tile_order):
    outputs = [one_block(rows[section_id], queries[section_id], keys[section_id], values[section_id], text_kv[section_id], text_count[section_id], out_weight[section_id], gate[section_id], band, tile_order) for section_id in range(SECTIONS)]
    return jnp.stack([outputs[(section_id - 1) % SECTIONS] for section_id in range(SECTIONS)], axis=0)
```

```python
import math

import jax
import jax.numpy as jnp
from jax import lax
from jax.experimental import pallas as pl
from jax.experimental.pallas import tpu as pltpu
from jax.sharding import PartitionSpec as P

HD = 128
TILE = 128
BLOCK = 256
PAIR = 2 * BLOCK
CHIPS = 4
FAR = -30000.0
EXP2_SCALE = HD ** (-0.5) * math.log2(math.e)
BF16 = jnp.bfloat16
F32 = jnp.float32
SMEM = pl.BlockSpec(memory_space=pltpu.SMEM)
VMEM = pl.BlockSpec(memory_space=pltpu.VMEM)
ANY = pl.BlockSpec(memory_space=pl.ANY)


def params():
    return pltpu.CompilerParams(vmem_limit_bytes=32 * 1024 * 1024)


def normed(block):
    wide = block.astype(F32)
    return (wide * lax.rsqrt(jnp.mean(wide * wide, axis=-1, keepdims=True) + 1e-06)).astype(BF16)


def split_heads(place, q_ref, k_ref, v_ref, pair_ref, near_ref, cross_ref, mine_ref):
    first = place[1] == 0

    def pick(a, b):
        return jnp.where(first, a, b)

    def halves(ref, prepare):
        a = prepare(ref[0, :, :HD])
        b = prepare(ref[0, :, HD:])
        return pick(a, b), pick(b, a)

    key_own, key_other = halves(k_ref, normed)
    value_own, value_other = halves(v_ref, lambda x: x)
    query_own, query_other = halves(q_ref, normed)
    pair_ref[0] = key_other
    pair_ref[1] = value_other
    pair_ref[2] = query_other
    cross_ref[0] = key_other
    cross_ref[1] = value_other
    near_ref[0] = key_own
    near_ref[1] = value_own
    mine_ref[...] = query_own


def regroup(place, w_ref, t_ref, own_ref, one_ref, two_ref, three_ref, text_ref, sems):
    chip, core, odd = place[2], place[3], place[1]
    width = w_ref.shape[2] // (2 * CHIPS)
    copies = []
    for ahead, out in enumerate((own_ref, one_ref, two_ref, three_ref)):
        target = lax.rem(chip + ahead, CHIPS)
        for half in range(2):
            side = core if half == 0 else 1 - core
            start = pl.multiple_of((target * 2 + side) * width, 128)
            copies.append((w_ref.at[0, :, pl.ds(start, width)], out.at[:, pl.ds(half * width, width)]))
    for group in range(2 * CHIPS):
        start = pl.multiple_of((2 * group + odd) * HD, 128)
        copies.append((t_ref.at[0, :, :, pl.ds(start, HD)], text_ref.at[group]))
    started = [
        pltpu.make_async_copy(source, target, sems.at[i])
        for i, (source, target) in enumerate(copies)
    ]
    for copy in started:
        copy.start()
    for copy in started:
        copy.wait()


def tile_at(place, order, pair, slot):
    return order[pair * 4 + ((slot // 2) ^ place[1]) * 2 + slot % 2]


def mask_lanes(place, order, band, pairs, text_lane):
    total = order.shape[0] // 4
    lane = lax.broadcasted_iota(jnp.int32, (TILE, HD), 1)
    key_tiles = []
    for pair in pairs:
        inside = (pair >= 0) & (pair < total)
        held = jnp.clip(pair, 0, total - 1)
        key_tiles += [(inside, tile_at(place, order, held, slot)) for slot in range(4)]
    rows = []
    for slot in range(4):
        tile = tile_at(place, order, place[0], slot)
        low, high = band[tile, 0], band[tile, 1]
        row = jnp.where(lane == text_lane, F32(FAR), F32(0.0))
        for index, (inside, key_tile) in enumerate(key_tiles):
            seen = inside & (key_tile >= low) & (key_tile <= high)
            row = jnp.where(lane == index, jnp.where(seen, F32(0.0), F32(FAR)), row)
        rows.append(row.astype(BF16))
    return jnp.concatenate(rows, axis=0)


def add_keys(total, query, key, key_lanes, value):
    scores = lax.dot_general(
        query,
        jnp.concatenate([key, key_lanes], axis=1),
        (((1,), (1,)), ((), ())),
        preferred_element_type=F32,
    )
    weights = jnp.exp2(scores * EXP2_SCALE).astype(BF16)
    wide = jnp.concatenate([value, jnp.ones_like(value)], axis=1)
    part = lax.dot_general(weights, wide, (((1,), (0,)), ((), ())), preferred_element_type=F32)
    return part if total is None else total + part


def video_lanes(index):
    shape = (PAIR, HD)
    row = lax.broadcasted_iota(jnp.int32, shape, 0)
    lane = lax.broadcasted_iota(jnp.int32, shape, 1)
    return jnp.where(lane == 4 * index + row // TILE, F32(1.0), F32(0.0)).astype(BF16)


def pair_arrays(low_ref, high_ref):
    key = jnp.concatenate([low_ref[0], high_ref[0]], axis=0)
    value = jnp.concatenate([low_ref[1], high_ref[1]], axis=0)
    return key, value


def near_keys(
    place, order, band, count, mine_ref, near_ref, pair_ref, far_ref, cross_ref, text_ref, total_ref
):
    query = jnp.concatenate([mine_ref[...], pair_ref[2]], axis=0)
    pairs = (place[0], place[0] ^ 1)
    query = jnp.concatenate([query, mask_lanes(place, order, band, pairs, HD - 1)], axis=1)
    total = add_keys(None, query, *with_lanes(pair_arrays(near_ref, pair_ref), 0))
    total = add_keys(total, query, *with_lanes(pair_arrays(far_ref, cross_ref), 1))
    text = text_ref[...]
    slots = text.shape[0] * text.shape[2]
    text_key = normed(text[:, 0].reshape(slots, HD))
    text_value = text[:, 1].reshape(slots, HD)
    slot = lax.broadcasted_iota(jnp.int32, (slots, HD), 0)
    lane = lax.broadcasted_iota(jnp.int32, (slots, HD), 1)
    dead = (lane == HD - 1) & (slot >= count[0])
    text_lanes = jnp.where(dead, F32(1.0), F32(0.0)).astype(BF16)
    total_ref[...] = add_keys(total, query, text_key, text_lanes, text_value)


def with_lanes(arrays, index):
    key, value = arrays
    return key, video_lanes(index), value


def far_keys(
    place, order, band, mine_ref, pair_ref, total_ref, below_ref, above_ref, next_ref, out_ref
):
    query = jnp.concatenate([mine_ref[...], pair_ref[2]], axis=0)
    own = place[0]
    beside = own - 1 + 2 * lax.rem(own, 2)
    lanes = mask_lanes(place, order, band, (own - 2, own + 2, beside), -1)
    query = jnp.concatenate([query, lanes], axis=1)
    total = total_ref[...]
    for index, ref in enumerate((below_ref, above_ref, next_ref)):
        total = add_keys(total, query, *with_lanes(pair_arrays(ref.at[0], ref.at[1]), index))
    result = (total[:, :HD] / total[:, HD:]).astype(BF16)
    odd = place[1]
    for chip in range(CHIPS):
        out_ref[odd * CHIPS + chip] = result[:BLOCK]
        out_ref[(1 - odd) * CHIPS + chip] = result[BLOCK:]


def project(place, heads_ref, own_ref, one_ref, two_ref, three_ref, kept_ref, sent_ref):
    total = None
    for behind, weight_ref in enumerate((own_ref, one_ref, two_ref, three_ref)):
        source = lax.rem(place[2] + CHIPS - behind, CHIPS)
        heads = jnp.concatenate([heads_ref[source], heads_ref[CHIPS + source]], axis=1)
        part = jnp.dot(heads, weight_ref[...], preferred_element_type=F32)
        total = part if total is None else total + part
    width = kept_ref.shape[1]
    kept_ref[...] = total[:, :width]
    sent_ref[...] = total[:, width:].astype(BF16)


def body(rows, queries, keys, values, text_kv, text_count, out_weight, gate, band, tile_order):
    seq_count = lax.axis_size("seq")
    seq = lax.axis_index("seq")
    grp = lax.axis_index("grp")
    place = jnp.stack([seq // 2, seq % 2, grp // 2, grp % 2]).astype(jnp.int32)
    shape = jax.ShapeDtypeStruct
    width = gate.shape[1]

    pair_out, near, cross_out, mine = pl.pallas_call(
        split_heads,
        out_shape=(
            shape((3, BLOCK, HD), BF16),
            shape((2, BLOCK, HD), BF16),
            shape((2, BLOCK, HD), BF16),
            shape((BLOCK, HD), BF16),
        ),
        in_specs=[SMEM, VMEM, VMEM, VMEM],
        compiler_params=params(),
        cost_estimate=pl.CostEstimate(flops=10**6, bytes_accessed=10**6, transcendentals=0),
    )(place, queries, keys, values)

    def swapped(block, mask):
        return lax.ppermute(block, "seq", [(i, i ^ mask) for i in range(seq_count)])

    pair_in = swapped(pair_out, 1)
    far_in = swapped(near, 2)
    cross_in = swapped(cross_out, 3)

    blocks = [shape((BLOCK, 2 * width), BF16)] * CHIPS
    weight_own, *weight_out, text_out = pl.pallas_call(
        regroup,
        out_shape=(*blocks, shape((2 * CHIPS, 2, text_kv.shape[2], HD), BF16)),
        in_specs=[SMEM, ANY, ANY],
        out_specs=(ANY,) * 5,
        scratch_shapes=[pltpu.SemaphoreType.DMA((4 * CHIPS,))],
        compiler_params=params(),
        cost_estimate=pl.CostEstimate(flops=0, bytes_accessed=4 * 10**6, transcendentals=0),
    )(place, out_weight, text_kv)
    weight_in = [
        lax.ppermute(
            block,
            "grp",
            [(g, (g + 2 * (ahead + 1)) % (2 * CHIPS)) for g in range(2 * CHIPS)],
        )
        for ahead, block in enumerate(weight_out)
    ]
    text_in = lax.all_to_all(text_out, "grp", 0, 0)

    own_pair = jnp.stack([near, pair_in[:2]])
    other_pair = jnp.stack([far_in, cross_in])
    up = [(i, i + 4) for i in range(seq_count - 4)]
    down = [(i + 4, i) for i in range(seq_count - 4)]
    below = lax.ppermute(own_pair, "seq", up)
    above = lax.ppermute(own_pair, "seq", down)
    mixed = [(i, j) for i, j in up if i % 4 < 2] + [(i, j) for i, j in down if i % 4 >= 2]
    beside = lax.ppermute(other_pair, "seq", mixed)

    total = pl.pallas_call(
        near_keys,
        out_shape=shape((PAIR, 2 * HD), F32),
        in_specs=[SMEM] * 4 + [VMEM] * 6,
        compiler_params=params(),
        cost_estimate=pl.CostEstimate(
            flops=4 * PAIR * (2 * PAIR + 256) * 256, bytes_accessed=2 * 10**6, transcendentals=10**6
        ),
    )(place, tile_order, band, text_count, mine, near, pair_in, far_in, cross_in, text_in)
    attention = pl.pallas_call(
        far_keys,
        out_shape=shape((2 * CHIPS, BLOCK, HD), BF16),
        in_specs=[SMEM] * 3 + [VMEM] * 6,
        compiler_params=params(),
        cost_estimate=pl.CostEstimate(
            flops=4 * PAIR * 3 * PAIR * 256, bytes_accessed=2 * 10**6, transcendentals=10**6
        ),
    )(place, tile_order, band, mine, pair_in, total, below, above, beside)

    groups = [
        [(2 * pair + odd) * 2 * CHIPS + 2 * chip + core for odd in range(2) for chip in range(CHIPS)]
        for pair in range(seq_count // 2)
        for core in range(2)
    ]
    heads = lax.all_to_all(attention, ("seq", "grp"), 0, 0, axis_index_groups=groups)
    kept, sent = pl.pallas_call(
        project,
        out_shape=(shape((BLOCK, width), F32), shape((BLOCK, width), BF16)),
        in_specs=[SMEM] + [VMEM] * 5,
        compiler_params=params(),
        cost_estimate=pl.CostEstimate(
            flops=2 * BLOCK * 1024 * 768, bytes_accessed=3 * 10**6, transcendentals=0
        ),
    )(place, heads, weight_own, *weight_in)
    other = lax.ppermute(sent, "grp", [(g, g ^ 1) for g in range(2 * CHIPS)])
    share = kept + other.astype(F32)
    result = (rows[0].astype(F32) + gate[0][None, :] * share).astype(BF16)
    handed = lax.ppermute(result, "section", [(0, 1), (1, 0)])
    return handed[None]


def solution(mesh):
    placed = (
        P("section", "seq", "grp"),
        P("section", "seq", "grp"),
        P("section", "seq", "grp"),
        P("section", "seq", "grp"),
        P("section", None, "grp", None),
        P("section"),
        P("section", "grp", None),
        P("section", "grp"),
        P(),
        P(),
    )
    return jax.shard_map(
        body, mesh=mesh, in_specs=placed, out_specs=P("section", "seq", "grp"), check_vma=False
    )
```

```python
import math

import jax
import jax.numpy as jnp
from jax import lax
from jax.experimental import pallas as pl
from jax.experimental.pallas import tpu as pltpu
from jax.sharding import PartitionSpec as P

HD = 128
TILE = 128
BLOCK = 256
PAIR = 2 * BLOCK
CHIPS = 4
FAR = -30000.0
EXP2_SCALE = HD ** (-0.5) * math.log2(math.e)
BF16 = jnp.bfloat16
F32 = jnp.float32
SMEM = pl.BlockSpec(memory_space=pltpu.SMEM)
VMEM = pl.BlockSpec(memory_space=pltpu.VMEM)
ANY = pl.BlockSpec(memory_space=pl.ANY)
HBM = pl.BlockSpec(memory_space=pltpu.HBM)


def params(mib=32):
    return pltpu.CompilerParams(vmem_limit_bytes=mib * 1024 * 1024)


def normed(block):
    wide = block.astype(F32)
    return (wide * lax.rsqrt(jnp.mean(wide * wide, axis=-1, keepdims=True) + 1e-06)).astype(BF16)


def start_out(
    place, q_ref, k_ref, v_ref, w_ref, t_ref, spread_ref, pair_ref, near_ref, cross_ref, mine_ref,
    q_in, k_in, v_in, in_sems, out_sems,
):
    odd, chip, core = place[1], place[2], place[3]
    rows, width = w_ref.shape[1], w_ref.shape[2] // (2 * CHIPS)
    slots = t_ref.shape[2]
    loads = [
        pltpu.make_async_copy(source.at[0], target, in_sems.at[i])
        for i, (source, target) in enumerate(((k_ref, k_in), (v_ref, v_in), (q_ref, q_in)))
    ]
    for load in loads:
        load.start()
    copies = []
    for target in range(CHIPS):
        for half in range(2):
            side = target * 2 + (core if half == 0 else 1 - core)
            columns = pl.ds(pl.multiple_of(side * width, 128), width)
            copies.append((
                w_ref.at[0, :, columns],
                spread_ref.at[target, pl.ds(0, rows), pl.ds(half * width, width)],
            ))
            columns = pl.ds(pl.multiple_of((side * 2 + odd) * HD, 128), HD)
            for kind in range(2):
                copies.append((
                    t_ref.at[0, kind, :, columns],
                    spread_ref.at[target, pl.ds(rows, slots), pl.ds((2 * half + kind) * HD, HD)],
                ))
    copies = [
        pltpu.make_async_copy(source, target, out_sems.at[i])
        for i, (source, target) in enumerate(copies)
    ]
    for copy in copies:
        copy.start()

    def halves(load, ref, prepare):
        load.wait()
        a, b = prepare(ref[:, :HD]), prepare(ref[:, HD:])
        return jnp.where(odd == 0, a, b), jnp.where(odd == 0, b, a)

    key_own, key_other = halves(loads[0], k_in, normed)
    pair_ref[0] = key_other
    cross_ref[0] = key_other
    near_ref[0] = key_own
    value_own, value_other = halves(loads[1], v_in, lambda x: x)
    pair_ref[1] = value_other
    cross_ref[1] = value_other
    near_ref[1] = value_own
    query_own, query_other = halves(loads[2], q_in, normed)
    pair_ref[2] = query_other
    mine_ref[...] = query_own
    for copy in copies:
        copy.wait()


def tile_at(place, order, pair, slot):
    return order[pair * 4 + ((slot // 2) ^ place[1]) * 2 + slot % 2]


def mask_lanes(place, order, band, pairs, text_lane):
    total = order.shape[0] // 4
    lane = lax.broadcasted_iota(jnp.int32, (TILE, HD), 1)
    key_tiles = []
    for pair in pairs:
        inside = (pair >= 0) & (pair < total)
        held = jnp.clip(pair, 0, total - 1)
        key_tiles += [(inside, tile_at(place, order, held, slot)) for slot in range(4)]
    rows = []
    for slot in range(4):
        tile = tile_at(place, order, place[0], slot)
        low, high = band[tile, 0], band[tile, 1]
        row = jnp.where(lane == text_lane, F32(FAR), F32(0.0))
        for index, (inside, key_tile) in enumerate(key_tiles):
            seen = inside & (key_tile >= low) & (key_tile <= high)
            row = jnp.where(lane == index, jnp.where(seen, F32(0.0), F32(FAR)), row)
        rows.append(row.astype(BF16))
    return jnp.concatenate(rows, axis=0)


def add_keys(total, query, key, key_lanes, value):
    scores = lax.dot_general(
        query,
        jnp.concatenate([key, key_lanes], axis=1),
        (((1,), (1,)), ((), ())),
        preferred_element_type=F32,
    )
    weights = jnp.exp2(scores * EXP2_SCALE).astype(BF16)
    wide = jnp.concatenate([value, jnp.ones_like(value)], axis=1)
    part = lax.dot_general(weights, wide, (((1,), (0,)), ((), ())), preferred_element_type=F32)
    return part if total is None else total + part


def video_lanes(index):
    shape = (PAIR, HD)
    row = lax.broadcasted_iota(jnp.int32, shape, 0)
    lane = lax.broadcasted_iota(jnp.int32, shape, 1)
    return jnp.where(lane == 4 * index + row // TILE, F32(1.0), F32(0.0)).astype(BF16)


def pair_arrays(low_ref, high_ref):
    key = jnp.concatenate([low_ref[0], high_ref[0]], axis=0)
    value = jnp.concatenate([low_ref[1], high_ref[1]], axis=0)
    return key, value


def with_lanes(arrays, index):
    key, value = arrays
    return key, video_lanes(index), value


def masked_query(place, order, band, mine_ref, pair_ref, pairs, text_lane):
    query = jnp.concatenate([mine_ref[...], pair_ref[2]], axis=0)
    return jnp.concatenate([query, mask_lanes(place, order, band, pairs, text_lane)], axis=1)


def near_keys(place, order, band, mine_ref, near_ref, pair_ref, far_ref, cross_ref, total_ref):
    pairs = (place[0], place[0] ^ 1)
    query = masked_query(place, order, band, mine_ref, pair_ref, pairs, -1)
    total = add_keys(None, query, *with_lanes(pair_arrays(near_ref, pair_ref), 0))
    total_ref[...] = add_keys(total, query, *with_lanes(pair_arrays(far_ref, cross_ref), 1))


def text_arrays(text_ref, side, count):
    text = text_ref[...]
    chips, held, _ = text.shape
    key = normed(text[:, :, :HD].reshape(chips * held, HD))
    value = text[:, :, HD:].reshape(chips * held, HD)
    row = lax.broadcasted_iota(jnp.int32, key.shape, 0)
    lane = lax.broadcasted_iota(jnp.int32, key.shape, 1)
    slot = (2 * (row // held) + side) * held + row % held
    dead = (lane == HD - 1) & (slot >= count[0])
    return key, jnp.where(dead, F32(1.0), F32(0.0)).astype(BF16), value


def middle_keys(
    place, order, band, count, mine_ref, pair_ref, sum_ref, below_ref, above_ref, own_text, core_text,
    total_ref,
):
    pairs = (place[0] - 2, place[0] + 2)
    query = masked_query(place, order, band, mine_ref, pair_ref, pairs, HD - 1)
    total = sum_ref[...]
    for index, ref in enumerate((below_ref, above_ref)):
        total = add_keys(total, query, *with_lanes(pair_arrays(ref.at[0], ref.at[1]), index))
    total = add_keys(total, query, *text_arrays(own_text, place[3], count))
    total_ref[...] = add_keys(total, query, *text_arrays(core_text, 1 - place[3], count))


def last_keys(place, order, band, mine_ref, pair_ref, sum_ref, beside_ref, out_ref, held, sems):
    loads = [
        pltpu.make_async_copy(beside_ref.at[block, kind], held.at[kind, block], sems.at[kind, block])
        for kind in range(2)
        for block in range(2)
    ]
    for load in loads:
        load.start()
    own, odd = place[0], place[1]
    beside = own - 1 + 2 * lax.rem(own, 2)
    query = masked_query(place, order, band, mine_ref, pair_ref, (beside,), -1)
    for load in loads:
        load.wait()
    key = jnp.concatenate([held[0, 0], held[0, 1]], axis=0)
    value = jnp.concatenate([held[1, 0], held[1, 1]], axis=0)
    total = add_keys(sum_ref[...], query, key, video_lanes(0), value)
    result = (total[:, :HD] / total[:, HD:]).astype(BF16)
    for chip in range(CHIPS):
        out_ref[odd * CHIPS + chip] = result[BLOCK:]
        out_ref[(1 - odd) * CHIPS + chip] = result[:BLOCK]


def project(heads_ref, weight_ref, kept_ref, sent_ref):
    total = None
    depth = 2 * HD
    for chip in range(CHIPS):
        heads = jnp.concatenate([heads_ref[chip], heads_ref[CHIPS + chip]], axis=1)
        part = jnp.dot(heads, weight_ref[chip, :depth], preferred_element_type=F32)
        total = part if total is None else total + part
    width = kept_ref.shape[1]
    kept_ref[...] = total[:, :width]
    sent_ref[...] = total[:, width:].astype(BF16)


def body(rows, queries, keys, values, text_kv, text_count, out_weight, gate, band, tile_order):
    seq_count = lax.axis_size("seq")
    seq = lax.axis_index("seq")
    grp = lax.axis_index("grp")
    place = jnp.stack([seq // 2, seq % 2, grp // 2, grp % 2]).astype(jnp.int32)
    shape = jax.ShapeDtypeStruct
    width = gate.shape[1]
    depth, slots = out_weight.shape[1], text_kv.shape[2]

    spread, pair_out, near, cross_out, mine = pl.pallas_call(
        start_out,
        out_shape=(
            shape((CHIPS, depth + slots, 2 * width), BF16),
            shape((3, BLOCK, HD), BF16),
            shape((2, BLOCK, HD), BF16),
            shape((2, BLOCK, HD), BF16),
            shape((BLOCK, HD), BF16),
        ),
        in_specs=[SMEM] + [HBM] * 5,
        out_specs=(ANY,) + (VMEM,) * 4,
        scratch_shapes=[pltpu.VMEM((BLOCK, 2 * HD), BF16)] * 3
        + [pltpu.SemaphoreType.DMA((3,)), pltpu.SemaphoreType.DMA((6 * CHIPS,))],
        compiler_params=params(60),
        cost_estimate=pl.CostEstimate(flops=10**6, bytes_accessed=4 * 10**6, transcendentals=0),
    )(place, queries, keys, values, out_weight, text_kv)

    by_core = [[2 * chip + core for chip in range(CHIPS)] for core in range(2)]
    spread = lax.all_to_all(spread, "grp", 0, 0, axis_index_groups=by_core)

    def swapped(block, mask):
        return lax.ppermute(block, "seq", [(i, i ^ mask) for i in range(seq_count)])

    pair_in = swapped(pair_out, 1)
    far_in = swapped(near, 2)
    cross_in = swapped(cross_out, 3)
    rows_in = swapped(rows[0], 1)

    own_pair = jnp.stack([near, pair_in[:2]])
    other_pair = jnp.stack([far_in, cross_in])
    up = [(i, i + 4) for i in range(seq_count - 4)]
    down = [(i + 4, i) for i in range(seq_count - 4)]
    below = lax.ppermute(own_pair, "seq", up)
    above = lax.ppermute(own_pair, "seq", down)
    mixed = [(i, j) for i, j in up if i % 4 < 2] + [(i, j) for i, j in down if i % 4 >= 2]
    beside = lax.ppermute(other_pair, "seq", mixed)

    def cost(pieces):
        size = 4 * PAIR * pieces * PAIR * 256
        return pl.CostEstimate(flops=size, bytes_accessed=10**6, transcendentals=PAIR * pieces * PAIR)

    sums = shape((PAIR, 2 * HD), F32)
    total = pl.pallas_call(
        near_keys,
        out_shape=sums,
        in_specs=[SMEM] * 3 + [VMEM] * 5,
        compiler_params=params(),
        cost_estimate=cost(2),
    )(place, tile_order, band, mine, near, pair_in, far_in, cross_in)
    total, rows_in, spread = lax.optimization_barrier((total, rows_in, spread))
    own_text = spread[:, depth:, : 2 * HD]
    core_text = lax.ppermute(
        spread[:, depth:, 2 * HD : 4 * HD], "grp", [(g, g ^ 1) for g in range(2 * CHIPS)]
    )
    total = pl.pallas_call(
        middle_keys,
        out_shape=sums,
        in_specs=[SMEM] * 4 + [VMEM] * 7,
        compiler_params=params(),
        cost_estimate=cost(2),
    )(place, tile_order, band, text_count, mine, pair_in, total, below, above, own_text, core_text)
    attention = pl.pallas_call(
        last_keys,
        out_shape=shape((2 * CHIPS, BLOCK, HD), BF16),
        in_specs=[SMEM] * 3 + [VMEM] * 3 + [ANY],
        scratch_shapes=[pltpu.VMEM((2, 2, BLOCK, HD), BF16), pltpu.SemaphoreType.DMA((2, 2))],
        compiler_params=params(),
        cost_estimate=cost(1),
    )(place, tile_order, band, mine, pair_in, total, beside)

    groups = [
        [(2 * pair + odd) * 2 * CHIPS + 2 * chip + core for odd in range(2) for chip in range(CHIPS)]
        for pair in range(seq_count // 2)
        for core in range(2)
    ]
    heads = lax.all_to_all(attention, ("seq", "grp"), 0, 0, axis_index_groups=groups)
    kept, sent = pl.pallas_call(
        project,
        out_shape=(shape((BLOCK, width), F32), shape((BLOCK, width), BF16)),
        in_specs=[VMEM] * 2,
        compiler_params=params(),
        cost_estimate=pl.CostEstimate(
            flops=2 * BLOCK * 1024 * 768, bytes_accessed=3 * 10**6, transcendentals=0
        ),
    )(heads, spread)
    other = lax.ppermute(sent, "grp", [(g, g ^ 1) for g in range(2 * CHIPS)])
    share = kept + other.astype(F32)
    result = (rows_in.astype(F32) + gate[0][None, :] * share).astype(BF16)
    across = [
        (part * seq_count + i, (1 - part) * seq_count + (i ^ 1))
        for part in range(2)
        for i in range(seq_count)
    ]
    handed = lax.ppermute(result, ("section", "seq"), across)
    return handed[None]


def solution(mesh):
    placed = (
        P("section", "seq", "grp"),
        P("section", "seq", "grp"),
        P("section", "seq", "grp"),
        P("section", "seq", "grp"),
        P("section", None, "grp", None),
        P("section"),
        P("section", "grp", None),
        P("section", "grp"),
        P(),
        P(),
    )
    return jax.shard_map(
        body, mesh=mesh, in_specs=placed, out_specs=P("section", "seq", "grp"), check_vma=False
    )
```

```python
import math

import jax
import jax.numpy as jnp
from jax import lax
from jax.experimental import pallas as pl
from jax.experimental.pallas import tpu as pltpu
from jax.sharding import PartitionSpec as P

HD = 128
TILE = 128
BLOCK = 256
PAIR = 2 * BLOCK
CHIPS = 4
FAR = -30000.0
EXP2_SCALE = HD ** (-0.5) * math.log2(math.e)
PIECES = 5
TEXT_LANE = 4 * PIECES
COUNT_LANE, ODD_LANE, CORE_LANE = 32, 33, 34
BF16 = jnp.bfloat16
F32 = jnp.float32
SMEM = pl.BlockSpec(memory_space=pltpu.SMEM)
VMEM = pl.BlockSpec(memory_space=pltpu.VMEM)
HBM = pl.BlockSpec(memory_space=pltpu.HBM)


def params(mib=16):
    return pltpu.CompilerParams(vmem_limit_bytes=mib * 1024 * 1024)


def normed(block):
    wide = block.astype(F32)
    return (wide * lax.rsqrt(jnp.mean(wide * wide, axis=-1, keepdims=True) + 1e-06)).astype(BF16)


def start_out(
    place, order, band, count, q_ref, k_ref, v_ref, r_ref, w_ref, t_ref,
    spread_ref, near_ref, cross_ref, along_ref, mine_ref, mask_ref,
    q_in, k_in, v_in, sems, w_sems,
):
    odd, core = place[1], place[3]
    depth, width = w_ref.shape[1], w_ref.shape[2] // (2 * CHIPS)
    slots = t_ref.shape[2]
    loads = [
        pltpu.make_async_copy(source.at[0], target, sems.at[i])
        for i, (source, target) in enumerate((
            (k_ref, k_in), (v_ref, v_in), (q_ref, q_in), (r_ref, along_ref.at[:, pl.ds(0, width)])
        ))
    ]
    copies = []
    for target in range(CHIPS):
        for half in range(2):
            side = target * 2 + (core if half == 0 else 1 - core)
            columns = pl.ds(pl.multiple_of(side * width, 128), width)
            copies.append((
                w_ref.at[0, :, columns],
                spread_ref.at[target, pl.ds(0, depth), pl.ds(half * width, width)],
            ))
            columns = pl.ds(pl.multiple_of((side * 2 + odd) * HD, 128), HD)
            for kind in range(2):
                copies.append((
                    t_ref.at[0, kind, :, columns],
                    spread_ref.at[target, pl.ds(depth, slots), pl.ds((2 * half + kind) * HD, HD)],
                ))
    copies = [
        pltpu.make_async_copy(source, target, w_sems.at[i])
        for i, (source, target) in enumerate(copies)
    ]
    for copy in loads + copies:
        copy.start()
    spread_ref[:, depth:, 4 * HD :] = jnp.zeros((CHIPS, slots, 2 * width - 4 * HD), BF16)
    mask_ref[...] = mask_rows(place, order, band, count)

    def halves(load, ref, prepare):
        load.wait()
        a, b = prepare(ref[:, :HD]), prepare(ref[:, HD:])
        return jnp.where(odd == 0, a, b), jnp.where(odd == 0, b, a)

    near_ref[0], cross_ref[0] = halves(loads[0], k_in, normed)
    near_ref[1], cross_ref[1] = halves(loads[1], v_in, lambda x: x)
    mine_ref[...], along_ref[:, width:] = halves(loads[2], q_in, normed)
    loads[3].wait()
    for copy in copies:
        copy.wait()


def mask_rows(place, order, band, count):
    own, odd = place[0], place[1]
    total = order.shape[0] // 4

    def tile_at(pair, slot):
        return order[pair * 4 + ((slot // 2) ^ odd) * 2 + slot % 2]

    lane = lax.broadcasted_iota(jnp.int32, (8, HD), 1)
    row = lax.broadcasted_iota(jnp.int32, (8, HD), 0)
    low = jnp.zeros((8, HD), jnp.int32)
    high = jnp.zeros((8, HD), jnp.int32)
    for slot in range(4):
        tile = tile_at(own, slot)
        low = jnp.where(row == slot, band[tile, 0], low)
        high = jnp.where(row == slot, band[tile, 1], high)
    held = jnp.full((8, HD), -1, jnp.int32)
    beside = own - 1 + 2 * lax.rem(own, 2)
    for piece, pair in enumerate((own, own ^ 1, own - 2, own + 2, beside)):
        inside = (pair >= 0) & (pair < total)
        kept = jnp.clip(pair, 0, total - 1)
        for slot in range(4):
            tile = jnp.where(inside, tile_at(kept, slot), -1)
            held = jnp.where(lane == 4 * piece + slot, tile, held)
    seen = (held >= low) & (held <= high)
    result = jnp.where((lane <= TEXT_LANE) & jnp.logical_not(seen), F32(FAR), F32(0.0))
    for at, value in ((COUNT_LANE, count[0]), (ODD_LANE, odd), (CORE_LANE, place[3])):
        result = jnp.where(lane == at, value.astype(F32), result)
    return result


def masked_query(mask_ref, mine_ref, along_ref):
    query = jnp.concatenate([mine_ref[...], along_ref[:, along_ref.shape[1] - HD :]], axis=0)
    lane = lax.broadcasted_iota(jnp.int32, (TILE, HD), 1)
    lanes = [
        jnp.where(lane <= TEXT_LANE, mask_ref[slot : slot + 1, :], F32(0.0)).astype(BF16)
        for slot in range(4)
    ]
    return jnp.concatenate([query, jnp.concatenate(lanes, axis=0)], axis=1)


def add_keys(total, query, key, key_lanes, value):
    scores = lax.dot_general(
        query,
        jnp.concatenate([key, key_lanes], axis=1),
        (((1,), (1,)), ((), ())),
        preferred_element_type=F32,
    )
    weights = jnp.exp2(scores * EXP2_SCALE).astype(BF16)
    wide = jnp.concatenate([value, jnp.ones_like(value)], axis=1)
    part = lax.dot_general(weights, wide, (((1,), (0,)), ((), ())), preferred_element_type=F32)
    return part if total is None else total + part


def piece_arrays(index, low_ref, high_ref):
    shape = (PAIR, HD)
    row = lax.broadcasted_iota(jnp.int32, shape, 0)
    lane = lax.broadcasted_iota(jnp.int32, shape, 1)
    lanes = jnp.where(lane == 4 * index + row // TILE, F32(1.0), F32(0.0)).astype(BF16)
    key = jnp.concatenate([low_ref[0], high_ref[0]], axis=0)
    value = jnp.concatenate([low_ref[1], high_ref[1]], axis=0)
    return key, lanes, value


def text_arrays(mask_ref, text_ref, other_core):
    text = text_ref[...]
    chips, held, _ = text.shape
    key = normed(text[:, :, :HD].reshape(chips * held, HD))
    value = text[:, :, HD:].reshape(chips * held, HD)
    row = lax.broadcasted_iota(jnp.int32, key.shape, 0)
    lane = lax.broadcasted_iota(jnp.int32, key.shape, 1)
    core = mask_ref[0:1, CORE_LANE : CORE_LANE + 1]
    side = 1.0 - core if other_core else core
    slot = (2 * (row // held) * held + row % held).astype(F32) + side * held
    dead = (lane == TEXT_LANE) & (slot >= mask_ref[0:1, COUNT_LANE : COUNT_LANE + 1])
    return key, jnp.where(dead, F32(1.0), F32(0.0)).astype(BF16), value


def first_keys(
    mask_ref, mine_ref, along_ref, near_ref, pair_ref, far_ref, cross_ref, below_ref, above_ref,
    own_text, core_text, total_ref,
):
    query = masked_query(mask_ref, mine_ref, along_ref)
    total = add_keys(None, query, *piece_arrays(0, near_ref, pair_ref))
    total = add_keys(total, query, *piece_arrays(1, far_ref, cross_ref))
    total = add_keys(total, query, *piece_arrays(2, below_ref.at[0], below_ref.at[1]))
    total = add_keys(total, query, *piece_arrays(3, above_ref.at[0], above_ref.at[1]))
    total = add_keys(total, query, *text_arrays(mask_ref, own_text, False))
    total_ref[...] = add_keys(total, query, *text_arrays(mask_ref, core_text, True))


def last_keys(mask_ref, mine_ref, along_ref, sum_ref, beside_ref, out_ref):
    query = masked_query(mask_ref, mine_ref, along_ref)
    pieces = piece_arrays(PIECES - 1, beside_ref.at[0], beside_ref.at[1])
    total = add_keys(sum_ref[...], query, *pieces)
    result = total[:, :HD] / total[:, HD:]
    odd = mask_ref[0:1, ODD_LANE : ODD_LANE + 1] > 0.5
    own, other = result[:BLOCK], result[BLOCK:]
    to_even = jnp.where(odd, own, other).astype(BF16)
    to_odd = jnp.where(odd, other, own).astype(BF16)
    for chip in range(CHIPS):
        out_ref[chip] = to_even
        out_ref[CHIPS + chip] = to_odd


def project(heads_ref, weight_ref, along_ref, gate_ref, kept_ref, sent_ref):
    total = None
    depth, width = 2 * HD, kept_ref.shape[1]
    for chip in range(CHIPS):
        heads = jnp.concatenate([heads_ref[chip], heads_ref[CHIPS + chip]], axis=1)
        part = jnp.dot(heads, weight_ref[chip, :depth], preferred_element_type=F32)
        total = part if total is None else total + part
    kept_ref[...] = along_ref[:, :width].astype(F32) + gate_ref[...] * total[:, :width]
    sent_ref[...] = total[:, width:].astype(BF16)


def body(rows, queries, keys, values, text_kv, text_count, out_weight, gate, band, tile_order):
    seq_count = lax.axis_size("seq")
    seq = lax.axis_index("seq")
    grp = lax.axis_index("grp")
    place = jnp.stack([seq >> 1, seq & 1, grp >> 1, grp & 1]).astype(jnp.int32)
    shape = jax.ShapeDtypeStruct
    width = gate.shape[1]
    depth, slots = out_weight.shape[1], text_kv.shape[2]

    spread, near, cross_out, along, mine, mask = pl.pallas_call(
        start_out,
        out_shape=(
            shape((CHIPS, depth + slots, 2 * width), BF16),
            shape((2, BLOCK, HD), BF16),
            shape((2, BLOCK, HD), BF16),
            shape((BLOCK, width + HD), BF16),
            shape((BLOCK, HD), BF16),
            shape((8, HD), F32),
        ),
        in_specs=[SMEM] * 4 + [HBM] * 6,
        out_specs=(VMEM,) * 6,
        scratch_shapes=[pltpu.VMEM((BLOCK, 2 * HD), BF16)] * 3
        + [pltpu.SemaphoreType.DMA((4,)), pltpu.SemaphoreType.DMA((6 * CHIPS,))],
        compiler_params=params(60),
        cost_estimate=pl.CostEstimate(flops=10**6, bytes_accessed=4 * 10**6, transcendentals=0),
    )(place, tile_order, band, text_count, queries, keys, values, rows, out_weight, text_kv)

    by_core = [[2 * chip + core for chip in range(CHIPS)] for core in range(2)]
    spread = lax.all_to_all(spread, "grp", 0, 0, axis_index_groups=by_core)

    def swapped(block, mask):
        return lax.ppermute(block, "seq", [(i, i ^ mask) for i in range(seq_count)])

    pair_in = swapped(cross_out, 1)
    far_in = swapped(near, 2)
    cross_in = swapped(cross_out, 3)
    along_in = swapped(along, 1)

    own_pair = jnp.stack([near, pair_in])
    other_pair = jnp.stack([far_in, cross_in])
    up = [(i, i + 4) for i in range(seq_count - 4)]
    down = [(i + 4, i) for i in range(seq_count - 4)]
    below = lax.ppermute(own_pair, "seq", up)
    above = lax.ppermute(own_pair, "seq", down)
    mixed = [(i, j) for i, j in up if i % 4 < 2] + [(i, j) for i, j in down if i % 4 >= 2]
    beside = lax.ppermute(other_pair, "seq", mixed)

    own_text = spread[:, depth:, : 2 * HD]
    core_text = lax.ppermute(
        spread[:, depth:, 2 * HD : 4 * HD], "grp", [(g, g ^ 1) for g in range(2 * CHIPS)]
    )

    def cost(pieces):
        size = 4 * PAIR * pieces * PAIR * 256
        return pl.CostEstimate(flops=size, bytes_accessed=10**6, transcendentals=PAIR * pieces * PAIR)

    total = pl.pallas_call(
        first_keys,
        out_shape=shape((PAIR, 2 * HD), F32),
        in_specs=[VMEM] * 11,
        compiler_params=params(),
        cost_estimate=cost(5),
    )(mask, mine, along_in, near, pair_in, far_in, cross_in, below, above, own_text, core_text)
    attention = pl.pallas_call(
        last_keys,
        out_shape=shape((2 * CHIPS, BLOCK, HD), BF16),
        in_specs=[VMEM] * 5,
        compiler_params=params(),
        cost_estimate=cost(1),
    )(mask, mine, along_in, total, beside)

    groups = [
        [(2 * pair + odd) * 2 * CHIPS + 2 * chip + core for odd in range(2) for chip in range(CHIPS)]
        for pair in range(seq_count // 2)
        for core in range(2)
    ]
    heads = lax.all_to_all(attention, ("seq", "grp"), 0, 0, axis_index_groups=groups)
    kept, sent = pl.pallas_call(
        project,
        out_shape=(shape((BLOCK, width), F32), shape((BLOCK, width), BF16)),
        in_specs=[VMEM] * 4,
        compiler_params=params(),
        cost_estimate=pl.CostEstimate(
            flops=2 * BLOCK * 1024 * 768, bytes_accessed=3 * 10**6, transcendentals=0
        ),
    )(heads, spread, along_in, gate)
    other = lax.ppermute(sent, "grp", [(g, g ^ 1) for g in range(2 * CHIPS)])
    result = (kept + gate * other.astype(F32)).astype(BF16)
    across = [
        (part * seq_count + i, (1 - part) * seq_count + (i ^ 1))
        for part in range(2)
        for i in range(seq_count)
    ]
    handed = lax.ppermute(result, ("section", "seq"), across)
    return handed[None]


def solution(mesh):
    placed = (
        P("section", "seq", "grp"),
        P("section", "seq", "grp"),
        P("section", "seq", "grp"),
        P("section", "seq", "grp"),
        P("section", None, "grp", None),
        P("section"),
        P("section", "grp", None),
        P("section", "grp"),
        P(),
        P(),
    )
    return jax.shard_map(
        body, mesh=mesh, in_specs=placed, out_specs=P("section", "seq", "grp"), check_vma=False
    )
```

```python
import math

import jax
import jax.numpy as jnp
from jax import lax
from jax.experimental import pallas as pl
from jax.experimental.pallas import tpu as pltpu
from jax.sharding import PartitionSpec as P

HD = 128
TILE = 128
BLOCK = 256
PAIR = 2 * BLOCK
CHIPS = 4
FAR = -30000.0
EXP2_SCALE = HD ** (-0.5) * math.log2(math.e)
PIECES = 5
TEXT_LANE = 4 * PIECES
COUNT_LANE, ODD_LANE, CORE_LANE = 32, 33, 34
BF16 = jnp.bfloat16
F32 = jnp.float32
SMEM = pl.BlockSpec(memory_space=pltpu.SMEM)
VMEM = pl.BlockSpec(memory_space=pltpu.VMEM)
HBM = pl.BlockSpec(memory_space=pltpu.HBM)


def params(mib=16):
    return pltpu.CompilerParams(vmem_limit_bytes=mib * 1024 * 1024)


def normed(block):
    wide = block.astype(F32)
    return (wide * lax.rsqrt(jnp.mean(wide * wide, axis=-1, keepdims=True) + 1e-06)).astype(BF16)


def start_out(
    pair, odd, chip, core, order, band, count, q_ref, k_ref, v_ref, w_ref, t_ref,
    spread_ref, near_ref, cross_ref, mine_ref, other_ref, mask_ref,
    q_in, k_in, v_in, stage, near, cross, mine, other, mask, sems, stage_sems, out_sems,
):
    odd, core = odd[0], core[0]
    depth, width = w_ref.shape[1], w_ref.shape[2] // (2 * CHIPS)
    slots = t_ref.shape[2]
    loads = [
        pltpu.make_async_copy(source.at[0], target, sems.at[i])
        for i, (source, target) in enumerate(((k_ref, k_in), (v_ref, v_in), (q_ref, q_in)))
    ]
    staged = []
    for target in range(CHIPS):
        parts = []
        for half in range(2):
            side = target * 2 + (core if half == 0 else 1 - core)
            columns = pl.ds(pl.multiple_of(side * width, 128), width)
            parts.append((
                w_ref.at[0, :, columns],
                stage.at[target, pl.ds(0, depth), pl.ds(half * width, width)],
            ))
            columns = pl.ds(pl.multiple_of((side * 2 + odd) * HD, 128), HD)
            for kind in range(2):
                parts.append((
                    t_ref.at[0, kind, :, columns],
                    stage.at[target, pl.ds(depth, slots), pl.ds((2 * half + kind) * HD, HD)],
                ))
        staged.append([
            pltpu.make_async_copy(source, to, stage_sems.at[target, i])
            for i, (source, to) in enumerate(parts)
        ])
    for load in loads:
        load.start()
    for parts in staged:
        for part in parts:
            part.start()
    stage[:, depth:, 4 * HD :] = jnp.zeros((CHIPS, slots, 2 * width - 4 * HD), BF16)
    sent = []

    def send(source, target):
        sent.append(pltpu.make_async_copy(source, target, out_sems.at[len(sent)]))
        sent[-1].start()

    mask[...] = mask_rows(pair[0], odd, core, order, band, count)
    send(mask, mask_ref)

    def halves(load, ref, prepare):
        load.wait()
        a, b = prepare(ref[:, :HD]), prepare(ref[:, HD:])
        return jnp.where(odd == 0, a, b), jnp.where(odd == 0, b, a)

    near[0], cross[0] = halves(loads[0], k_in, normed)
    near[1], cross[1] = halves(loads[1], v_in, lambda x: x)
    send(near, near_ref)
    send(cross, cross_ref)
    mine[...], other[...] = halves(loads[2], q_in, normed)
    send(mine, mine_ref)
    send(other, other_ref)
    for target, parts in enumerate(staged):
        for part in parts:
            part.wait()
        send(stage.at[target], spread_ref.at[target])
    for copy in sent:
        copy.wait()


def mask_rows(own, odd, core, order, band, count):
    total = order.shape[0] // 4

    def tile_at(pair, slot):
        return order[pair * 4 + ((slot // 2) ^ odd) * 2 + slot % 2]

    lane = lax.broadcasted_iota(jnp.int32, (8, HD), 1)
    row = lax.broadcasted_iota(jnp.int32, (8, HD), 0)
    low = jnp.zeros((8, HD), jnp.int32)
    high = jnp.zeros((8, HD), jnp.int32)
    for slot in range(4):
        tile = tile_at(own, slot)
        low = jnp.where(row == slot, band[0, tile], low)
        high = jnp.where(row == slot, band[1, tile], high)
    held = jnp.full((8, HD), -1, jnp.int32)
    beside = own - 1 + 2 * lax.rem(own, 2)
    for piece, pair in enumerate((own, own ^ 1, own - 2, own + 2, beside)):
        inside = (pair >= 0) & (pair < total)
        kept = jnp.clip(pair, 0, total - 1)
        for slot in range(4):
            tile = jnp.where(inside, tile_at(kept, slot), -1)
            held = jnp.where(lane == 4 * piece + slot, tile, held)
    seen = (held >= low) & (held <= high)
    result = jnp.where((lane <= TEXT_LANE) & jnp.logical_not(seen), F32(FAR), F32(0.0))
    for at, value in ((COUNT_LANE, count[0]), (ODD_LANE, odd), (CORE_LANE, core)):
        result = jnp.where(lane == at, value.astype(F32), result)
    return result


def masked_query(mask_ref, mine_ref, query_ref):
    query = jnp.concatenate([mine_ref[...], query_ref[...]], axis=0)
    lane = lax.broadcasted_iota(jnp.int32, (TILE, HD), 1)
    lanes = [
        jnp.where(lane <= TEXT_LANE, mask_ref[slot : slot + 1, :], F32(0.0)).astype(BF16)
        for slot in range(4)
    ]
    return jnp.concatenate([query, jnp.concatenate(lanes, axis=0)], axis=1)


def add_keys(total, query, key, key_lanes, value):
    scores = lax.dot_general(
        query,
        jnp.concatenate([key, key_lanes], axis=1),
        (((1,), (1,)), ((), ())),
        preferred_element_type=F32,
    )
    weights = jnp.exp2(scores * EXP2_SCALE).astype(BF16)
    wide = jnp.concatenate([value, jnp.ones_like(value)], axis=1)
    part = lax.dot_general(weights, wide, (((1,), (0,)), ((), ())), preferred_element_type=F32)
    return part if total is None else total + part


def piece_arrays(index, low_ref, high_ref):
    shape = (PAIR, HD)
    row = lax.broadcasted_iota(jnp.int32, shape, 0)
    lane = lax.broadcasted_iota(jnp.int32, shape, 1)
    lanes = jnp.where(lane == 4 * index + row // TILE, F32(1.0), F32(0.0)).astype(BF16)
    key = jnp.concatenate([low_ref[0], high_ref[0]], axis=0)
    value = jnp.concatenate([low_ref[1], high_ref[1]], axis=0)
    return key, lanes, value


def text_arrays(mask_ref, text_ref, other_core):
    text = text_ref[...]
    chips, held, _ = text.shape
    key = normed(text[:, :, :HD].reshape(chips * held, HD))
    value = text[:, :, HD:].reshape(chips * held, HD)
    row = lax.broadcasted_iota(jnp.int32, key.shape, 0)
    lane = lax.broadcasted_iota(jnp.int32, key.shape, 1)
    core = mask_ref[0:1, CORE_LANE : CORE_LANE + 1]
    side = 1.0 - core if other_core else core
    slot = (2 * (row // held) * held + row % held).astype(F32) + side * held
    dead = (lane == TEXT_LANE) & (slot >= mask_ref[0:1, COUNT_LANE : COUNT_LANE + 1])
    return key, jnp.where(dead, F32(1.0), F32(0.0)).astype(BF16), value


def first_keys(
    mask_ref, mine_ref, query_ref, near_ref, pair_ref, far_ref, cross_ref, below_ref, above_ref,
    own_text, core_text, total_ref,
):
    query = masked_query(mask_ref, mine_ref, query_ref)
    total = add_keys(None, query, *piece_arrays(0, near_ref, pair_ref))
    total = add_keys(total, query, *piece_arrays(1, far_ref, cross_ref))
    total = add_keys(total, query, *piece_arrays(2, below_ref.at[0], below_ref.at[1]))
    total = add_keys(total, query, *piece_arrays(3, above_ref.at[0], above_ref.at[1]))
    total = add_keys(total, query, *text_arrays(mask_ref, own_text, False))
    total_ref[...] = add_keys(total, query, *text_arrays(mask_ref, core_text, True))


def last_keys(mask_ref, mine_ref, query_ref, sum_ref, beside_ref, out_ref):
    query = masked_query(mask_ref, mine_ref, query_ref)
    pieces = piece_arrays(PIECES - 1, beside_ref.at[0], beside_ref.at[1])
    total = add_keys(sum_ref[...], query, *pieces)
    result = total[:, :HD] / total[:, HD:]
    odd = mask_ref[0:1, ODD_LANE : ODD_LANE + 1] > 0.5
    own, other = result[:BLOCK], result[BLOCK:]
    to_even = jnp.where(odd, own, other).astype(BF16)
    to_odd = jnp.where(odd, other, own).astype(BF16)
    for chip in range(CHIPS):
        out_ref[chip] = to_even
        out_ref[CHIPS + chip] = to_odd


def project(heads_ref, weight_ref, rows_ref, gate_ref, kept_ref, sent_ref):
    total = None
    depth, width = 2 * HD, kept_ref.shape[1]
    for chip in range(CHIPS):
        heads = jnp.concatenate([heads_ref[chip], heads_ref[CHIPS + chip]], axis=1)
        part = jnp.dot(heads, weight_ref[chip, :depth], preferred_element_type=F32)
        total = part if total is None else total + part
    kept_ref[...] = rows_ref[...].astype(F32) + gate_ref[...] * total[:, :width]
    sent_ref[...] = total[:, width:].astype(BF16)


def body(rows, queries, keys, values, text_kv, text_count, out_weight, gate, band, tile_order):
    seq_count = lax.axis_size("seq")
    seq = lax.axis_index("seq")
    grp = lax.axis_index("grp")
    place = [at.astype(jnp.int32).reshape(1) for at in (seq >> 1, seq & 1, grp >> 1, grp & 1)]
    shape = jax.ShapeDtypeStruct
    width = gate.shape[1]
    depth, slots = out_weight.shape[1], text_kv.shape[2]

    spread_shape = (CHIPS, depth + slots, 2 * width)
    token_shapes = [(2, BLOCK, HD)] * 2 + [(BLOCK, HD)] * 2
    spread, near, cross_out, mine, query_out, mask = pl.pallas_call(
        start_out,
        out_shape=[shape(dims, BF16) for dims in [spread_shape, *token_shapes]]
        + [shape((8, HD), F32)],
        in_specs=[SMEM] * 7 + [HBM] * 5,
        out_specs=[HBM] * 6,
        scratch_shapes=[pltpu.VMEM((BLOCK, 2 * HD), BF16)] * 3
        + [pltpu.VMEM(dims, BF16) for dims in [spread_shape, *token_shapes]]
        + [pltpu.VMEM((8, HD), F32)]
        + [pltpu.SemaphoreType.DMA(dims) for dims in ((3,), (CHIPS, 6), (5 + CHIPS,))],
        compiler_params=params(60),
        cost_estimate=pl.CostEstimate(flops=10**6, bytes_accessed=4 * 10**6, transcendentals=0),
    )(*place, tile_order, band.T, text_count, queries, keys, values, out_weight, text_kv)

    by_core = [[2 * chip + core for chip in range(CHIPS)] for core in range(2)]
    spread = lax.all_to_all(spread, "grp", 0, 0, axis_index_groups=by_core)

    def swapped(block, mask):
        return lax.ppermute(block, "seq", [(i, i ^ mask) for i in range(seq_count)])

    pair_in = swapped(cross_out, 1)
    far_in = swapped(near, 2)
    cross_in = swapped(cross_out, 3)

    own_pair = jnp.stack([near, pair_in])
    other_pair = jnp.stack([far_in, cross_in])
    other_pair, query_out = lax.optimization_barrier((other_pair, query_out))
    query_in = swapped(query_out, 1)
    up = [(i, i + 4) for i in range(seq_count - 4)]
    down = [(i + 4, i) for i in range(seq_count - 4)]
    below = lax.ppermute(own_pair, "seq", up)
    above = lax.ppermute(own_pair, "seq", down)
    mixed = [(i, j) for i, j in up if i % 4 < 2] + [(i, j) for i, j in down if i % 4 >= 2]
    beside = lax.ppermute(other_pair, "seq", mixed)

    own_text = spread[:, depth:, : 2 * HD]
    core_text = lax.ppermute(
        spread[:, depth:, 2 * HD : 4 * HD], "grp", [(g, g ^ 1) for g in range(2 * CHIPS)]
    )

    def cost(pieces):
        size = 4 * PAIR * pieces * PAIR * 256
        return pl.CostEstimate(flops=size, bytes_accessed=10**6, transcendentals=PAIR * pieces * PAIR)

    total = pl.pallas_call(
        first_keys,
        out_shape=shape((PAIR, 2 * HD), F32),
        in_specs=[VMEM] * 11,
        compiler_params=params(),
        cost_estimate=cost(5),
    )(mask, mine, query_in, near, pair_in, far_in, cross_in, below, above, own_text, core_text)
    total, rows_out = lax.optimization_barrier((total, rows[0]))
    rows_in = swapped(rows_out, 1)
    attention = pl.pallas_call(
        last_keys,
        out_shape=shape((2 * CHIPS, BLOCK, HD), BF16),
        in_specs=[VMEM] * 5,
        compiler_params=params(),
        cost_estimate=cost(1),
    )(mask, mine, query_in, total, beside)

    groups = [
        [(2 * pair + odd) * 2 * CHIPS + 2 * chip + core for odd in range(2) for chip in range(CHIPS)]
        for pair in range(seq_count // 2)
        for core in range(2)
    ]
    heads = lax.all_to_all(attention, ("seq", "grp"), 0, 0, axis_index_groups=groups)
    kept, sent = pl.pallas_call(
        project,
        out_shape=(shape((BLOCK, width), F32), shape((BLOCK, width), BF16)),
        in_specs=[VMEM] * 4,
        compiler_params=params(),
        cost_estimate=pl.CostEstimate(
            flops=2 * BLOCK * 1024 * 768, bytes_accessed=3 * 10**6, transcendentals=0
        ),
    )(heads, spread, rows_in, gate)
    other = lax.ppermute(sent, "grp", [(g, g ^ 1) for g in range(2 * CHIPS)])
    result = (kept + gate * other.astype(F32)).astype(BF16)
    across = [
        (part * seq_count + i, (1 - part) * seq_count + (i ^ 1))
        for part in range(2)
        for i in range(seq_count)
    ]
    handed = lax.ppermute(result, ("section", "seq"), across)
    return handed[None]


def solution(mesh):
    placed = (
        P("section", "seq", "grp"),
        P("section", "seq", "grp"),
        P("section", "seq", "grp"),
        P("section", "seq", "grp"),
        P("section", None, "grp", None),
        P("section"),
        P("section", "grp", None),
        P("section", "grp"),
        P(),
        P(),
    )
    return jax.shard_map(
        body, mesh=mesh, in_specs=placed, out_specs=P("section", "seq", "grp"), check_vma=False
    )
```

```python
import math

import jax
import jax.numpy as jnp
from jax import lax
from jax.experimental import pallas as pl
from jax.experimental.pallas import tpu as pltpu
from jax.sharding import PartitionSpec as P

HD = 128
TILE = 128
BLOCK = 256
PAIR = 2 * BLOCK
CHIPS = 4
FAR = -30000.0
EXP2_SCALE = HD ** (-0.5) * math.log2(math.e)
PIECES = 5
TEXT_LANE = 4 * PIECES
COUNT_LANE, ODD_LANE, CORE_LANE = 32, 33, 34
BF16 = jnp.bfloat16
F32 = jnp.float32
SMEM = pl.BlockSpec(memory_space=pltpu.SMEM)
VMEM = pl.BlockSpec(memory_space=pltpu.VMEM)
HBM = pl.BlockSpec(memory_space=pltpu.HBM)


def params(mib=16):
    return pltpu.CompilerParams(vmem_limit_bytes=mib * 1024 * 1024)


def normed(block):
    wide = block.astype(F32)
    return (wide * lax.rsqrt(jnp.mean(wide * wide, axis=-1, keepdims=True) + 1e-06)).astype(BF16)


def start_out(
    pair, odd, chip, core, order, band, count, q_ref, k_ref, v_ref, r_ref, w_ref, t_ref,
    spread_ref, near_ref, cross_ref, mine_ref, along_ref, mask_ref,
    q_in, k_in, v_in, t_in, stage, near, cross, mine, along, mask, sems, out_sems,
):
    odd, core = odd[0], core[0]
    depth, slots = w_ref.shape[1], t_ref.shape[2]
    width = w_ref.shape[2] // CHIPS
    loads = [
        (k_ref.at[0], k_in),
        (v_ref.at[0], v_in),
        (q_ref.at[0], q_in),
        (t_ref.at[0], t_in),
        (r_ref.at[0], along.at[:, pl.ds(0, r_ref.shape[2])]),
    ]
    loads += [
        (w_ref.at[0, :, pl.ds(target * width, width)], stage.at[target, pl.ds(0, depth)])
        for target in range(CHIPS)
    ]
    loads = [
        pltpu.make_async_copy(source, target, sems.at[i])
        for i, (source, target) in enumerate(loads)
    ]
    for load in loads:
        load.start()
    sent = []

    def send(source, target):
        sent.append(pltpu.make_async_copy(source, target, out_sems.at[len(sent)]))
        sent[-1].start()

    mask[...] = mask_rows(pair[0], odd, core, order, band, count)
    send(mask, mask_ref)

    def halves(load, ref, prepare):
        load.wait()
        a, b = prepare(ref[:, :HD]), prepare(ref[:, HD:])
        return jnp.where(odd == 0, a, b), jnp.where(odd == 0, b, a)

    near[0], cross[0] = halves(loads[0], k_in, normed)
    near[1], cross[1] = halves(loads[1], v_in, lambda x: x)
    send(near, near_ref)
    send(cross, cross_ref)
    mine[...], along[:, r_ref.shape[2] :] = halves(loads[2], q_in, normed)
    send(mine, mine_ref)
    loads[3].wait()
    for target in range(CHIPS):
        panels = []
        for kind in range(2):
            one, two = (
                jnp.where(odd == 0, t_in[kind, :, at : at + HD], t_in[kind, :, at + HD : at + 2 * HD])
                for at in (4 * target * HD, (4 * target + 2) * HD)
            )
            panels.append((jnp.where(core == 0, one, two), jnp.where(core == 0, two, one)))
        for at, panel in enumerate((panels[0][0], panels[1][0], panels[0][1], panels[1][1])):
            stage[target, depth:, at * HD : (at + 1) * HD] = panel
        stage[target, depth:, 4 * HD :] = jnp.zeros((slots, width - 4 * HD), BF16)
    for target, load in enumerate(loads[5:]):
        load.wait()
        send(stage.at[target], spread_ref.at[target])
    loads[4].wait()
    send(along, along_ref)
    for copy in sent:
        copy.wait()


def mask_rows(own, odd, core, order, band, count):
    total = order.shape[0] // 4

    def tile_at(pair, slot):
        return order[pair * 4 + ((slot // 2) ^ odd) * 2 + slot % 2]

    lane = lax.broadcasted_iota(jnp.int32, (8, HD), 1)
    row = lax.broadcasted_iota(jnp.int32, (8, HD), 0)
    low = jnp.zeros((8, HD), jnp.int32)
    high = jnp.zeros((8, HD), jnp.int32)
    for slot in range(4):
        tile = tile_at(own, slot)
        low = jnp.where(row == slot, band[0, tile], low)
        high = jnp.where(row == slot, band[1, tile], high)
    held = jnp.full((8, HD), -1, jnp.int32)
    beside = own - 1 + 2 * lax.rem(own, 2)
    for piece, pair in enumerate((own, own ^ 1, own - 2, own + 2, beside)):
        inside = (pair >= 0) & (pair < total)
        kept = jnp.clip(pair, 0, total - 1)
        for slot in range(4):
            tile = jnp.where(inside, tile_at(kept, slot), -1)
            held = jnp.where(lane == 4 * piece + slot, tile, held)
    seen = (held >= low) & (held <= high)
    result = jnp.where((lane <= TEXT_LANE) & jnp.logical_not(seen), F32(FAR), F32(0.0))
    for at, value in ((COUNT_LANE, count[0]), (ODD_LANE, odd), (CORE_LANE, core)):
        result = jnp.where(lane == at, value.astype(F32), result)
    return result


def masked_query(mask_ref, mine_ref, along_ref):
    query = jnp.concatenate([mine_ref[...], along_ref[:, along_ref.shape[1] - HD :]], axis=0)
    lane = lax.broadcasted_iota(jnp.int32, (TILE, HD), 1)
    lanes = [
        jnp.where(lane <= TEXT_LANE, mask_ref[slot : slot + 1, :], F32(0.0)).astype(BF16)
        for slot in range(4)
    ]
    return jnp.concatenate([query, jnp.concatenate(lanes, axis=0)], axis=1)


def add_keys(total, query, key, key_lanes, value):
    scores = lax.dot_general(
        query,
        jnp.concatenate([key, key_lanes], axis=1),
        (((1,), (1,)), ((), ())),
        preferred_element_type=F32,
    )
    weights = jnp.exp2(scores * EXP2_SCALE).astype(BF16)
    wide = jnp.concatenate([value, jnp.ones_like(value)], axis=1)
    part = lax.dot_general(weights, wide, (((1,), (0,)), ((), ())), preferred_element_type=F32)
    return part if total is None else total + part


def piece_arrays(index, low_ref, high_ref):
    shape = (PAIR, HD)
    row = lax.broadcasted_iota(jnp.int32, shape, 0)
    lane = lax.broadcasted_iota(jnp.int32, shape, 1)
    lanes = jnp.where(lane == 4 * index + row // TILE, F32(1.0), F32(0.0)).astype(BF16)
    key = jnp.concatenate([low_ref[0], high_ref[0]], axis=0)
    value = jnp.concatenate([low_ref[1], high_ref[1]], axis=0)
    return key, lanes, value


def text_arrays(mask_ref, text_ref, other_core):
    text = text_ref[...]
    chips, held, _ = text.shape
    key = normed(text[:, :, :HD].reshape(chips * held, HD))
    value = text[:, :, HD:].reshape(chips * held, HD)
    row = lax.broadcasted_iota(jnp.int32, key.shape, 0)
    lane = lax.broadcasted_iota(jnp.int32, key.shape, 1)
    core = mask_ref[0:1, CORE_LANE : CORE_LANE + 1]
    side = 1.0 - core if other_core else core
    slot = (2 * (row // held) * held + row % held).astype(F32) + side * held
    dead = (lane == TEXT_LANE) & (slot >= mask_ref[0:1, COUNT_LANE : COUNT_LANE + 1])
    return key, jnp.where(dead, F32(1.0), F32(0.0)).astype(BF16), value


def first_keys(
    mask_ref, mine_ref, along_ref, near_ref, pair_ref, far_ref, cross_ref, below_ref, above_ref,
    own_text, core_text, total_ref,
):
    query = masked_query(mask_ref, mine_ref, along_ref)
    total = add_keys(None, query, *piece_arrays(0, near_ref, pair_ref))
    total = add_keys(total, query, *piece_arrays(1, far_ref, cross_ref))
    total = add_keys(total, query, *piece_arrays(2, below_ref.at[0], below_ref.at[1]))
    total = add_keys(total, query, *piece_arrays(3, above_ref.at[0], above_ref.at[1]))
    total = add_keys(total, query, *text_arrays(mask_ref, own_text, False))
    total_ref[...] = add_keys(total, query, *text_arrays(mask_ref, core_text, True))


def last_keys(mask_ref, mine_ref, along_ref, sum_ref, beside_ref, out_ref):
    query = masked_query(mask_ref, mine_ref, along_ref)
    pieces = piece_arrays(PIECES - 1, beside_ref.at[0], beside_ref.at[1])
    total = add_keys(sum_ref[...], query, *pieces)
    result = total[:, :HD] / total[:, HD:]
    odd = mask_ref[0:1, ODD_LANE : ODD_LANE + 1] > 0.5
    own, other = result[:BLOCK], result[BLOCK:]
    to_even = jnp.where(odd, own, other).astype(BF16)
    to_odd = jnp.where(odd, other, own).astype(BF16)
    for chip in range(CHIPS):
        out_ref[chip] = to_even
        out_ref[CHIPS + chip] = to_odd


def project(core, heads_ref, weight_ref, along_ref, gate_ref, kept_ref, sent_ref):
    total = None
    depth, width = 2 * HD, kept_ref.shape[1]
    for chip in range(CHIPS):
        heads = jnp.concatenate([heads_ref[chip], heads_ref[CHIPS + chip]], axis=1)
        part = jnp.dot(heads, weight_ref[chip, :depth], preferred_element_type=F32)
        total = part if total is None else total + part
    low, high = total[:, :width], total[:, width:]
    first = core[0] == 0
    kept = jnp.where(first, low, high)
    kept_ref[...] = along_ref[:, :width].astype(F32) + gate_ref[...] * kept
    sent_ref[...] = jnp.where(first, high, low).astype(BF16)


def body(rows, queries, keys, values, text_kv, text_count, out_weight, gate, band, tile_order):
    seq_count = lax.axis_size("seq")
    seq = lax.axis_index("seq")
    grp = lax.axis_index("grp")
    place = [at.astype(jnp.int32).reshape(1) for at in (seq >> 1, seq & 1, grp >> 1, grp & 1)]
    shape = jax.ShapeDtypeStruct
    width = gate.shape[1]
    depth, slots = out_weight.shape[1], text_kv.shape[2]

    spread_shape = (CHIPS, depth + slots, 2 * width)
    token_shapes = [(2, BLOCK, HD)] * 2 + [(BLOCK, HD), (BLOCK, width + HD)]
    spread, near, cross_out, mine, along, mask = pl.pallas_call(
        start_out,
        out_shape=[shape(dims, BF16) for dims in [spread_shape, *token_shapes]]
        + [shape((8, HD), F32)],
        in_specs=[SMEM] * 7 + [HBM] * 6,
        out_specs=[HBM] * 6,
        scratch_shapes=[pltpu.VMEM((BLOCK, 2 * HD), BF16)] * 3
        + [pltpu.VMEM(dims, BF16) for dims in [text_kv.shape[1:], spread_shape, *token_shapes]]
        + [pltpu.VMEM((8, HD), F32)]
        + [pltpu.SemaphoreType.DMA(dims) for dims in ((5 + CHIPS,), (5 + CHIPS,))],
        compiler_params=params(60),
        cost_estimate=pl.CostEstimate(flops=10**6, bytes_accessed=4 * 10**6, transcendentals=0),
    )(*place, tile_order, band.T, text_count, queries, keys, values, rows, out_weight, text_kv)

    by_core = [[2 * chip + core for chip in range(CHIPS)] for core in range(2)]
    spread = lax.all_to_all(spread, "grp", 0, 0, axis_index_groups=by_core)

    def swapped(block, mask):
        return lax.ppermute(block, "seq", [(i, i ^ mask) for i in range(seq_count)])

    pair_in = swapped(cross_out, 1)
    far_in = swapped(near, 2)
    cross_in = swapped(cross_out, 3)

    own_pair = jnp.stack([near, pair_in])
    other_pair = jnp.stack([far_in, cross_in])
    own_pair, along = lax.optimization_barrier((own_pair, along))
    along_in = swapped(along, 1)
    up = [(i, i + 4) for i in range(seq_count - 4)]
    down = [(i + 4, i) for i in range(seq_count - 4)]
    below = lax.ppermute(own_pair, "seq", up)
    above = lax.ppermute(own_pair, "seq", down)
    mixed = [(i, j) for i, j in up if i % 4 < 2] + [(i, j) for i, j in down if i % 4 >= 2]
    beside = lax.ppermute(other_pair, "seq", mixed)

    own_text = spread[:, depth:, : 2 * HD]
    core_text = lax.ppermute(
        spread[:, depth:, 2 * HD : 4 * HD], "grp", [(g, g ^ 1) for g in range(2 * CHIPS)]
    )

    def cost(pieces):
        size = 4 * PAIR * pieces * PAIR * 256
        return pl.CostEstimate(flops=size, bytes_accessed=10**6, transcendentals=PAIR * pieces * PAIR)

    total = pl.pallas_call(
        first_keys,
        out_shape=shape((PAIR, 2 * HD), F32),
        in_specs=[VMEM] * 11,
        compiler_params=params(),
        cost_estimate=cost(5),
    )(mask, mine, along_in, near, pair_in, far_in, cross_in, below, above, own_text, core_text)
    attention = pl.pallas_call(
        last_keys,
        out_shape=shape((2 * CHIPS, BLOCK, HD), BF16),
        in_specs=[VMEM] * 5,
        compiler_params=params(),
        cost_estimate=cost(1),
    )(mask, mine, along_in, total, beside)

    groups = [
        [(2 * pair + odd) * 2 * CHIPS + 2 * chip + core for odd in range(2) for chip in range(CHIPS)]
        for pair in range(seq_count // 2)
        for core in range(2)
    ]
    heads = lax.all_to_all(attention, ("seq", "grp"), 0, 0, axis_index_groups=groups)
    kept, sent = pl.pallas_call(
        project,
        out_shape=(shape((BLOCK, width), F32), shape((BLOCK, width), BF16)),
        in_specs=[SMEM] + [VMEM] * 4,
        compiler_params=params(),
        cost_estimate=pl.CostEstimate(
            flops=2 * BLOCK * 1024 * 768, bytes_accessed=3 * 10**6, transcendentals=0
        ),
    )(place[3], heads, spread, along_in, gate)
    other = lax.ppermute(sent, "grp", [(g, g ^ 1) for g in range(2 * CHIPS)])
    result = (kept + gate * other.astype(F32)).astype(BF16)
    across = [
        (part * seq_count + i, (1 - part) * seq_count + (i ^ 1))
        for part in range(2)
        for i in range(seq_count)
    ]
    handed = lax.ppermute(result, ("section", "seq"), across)
    return handed[None]


def solution(mesh):
    placed = (
        P("section", "seq", "grp"),
        P("section", "seq", "grp"),
        P("section", "seq", "grp"),
        P("section", "seq", "grp"),
        P("section", None, "grp", None),
        P("section"),
        P("section", "grp", None),
        P("section", "grp"),
        P(),
        P(),
    )
    return jax.shard_map(
        body, mesh=mesh, in_specs=placed, out_specs=P("section", "seq", "grp"), check_vma=False
    )
```

```python
import math

import jax
import jax.numpy as jnp
from jax import lax
from jax.experimental import pallas as pl
from jax.experimental.pallas import tpu as pltpu
from jax.sharding import PartitionSpec as P

HD = 128
TILE = 128
BLOCK = 256
PAIR = 2 * BLOCK
CHIPS = 4
FAR = -30000.0
EXP2_SCALE = HD ** (-0.5) * math.log2(math.e)
PIECES = 5
TEXT_LANE = 4 * PIECES
COUNT_LANE, ODD_LANE, CORE_LANE = 32, 33, 34
BF16 = jnp.bfloat16
F32 = jnp.float32
SMEM = pl.BlockSpec(memory_space=pltpu.SMEM)
VMEM = pl.BlockSpec(memory_space=pltpu.VMEM)
ANY = pl.BlockSpec(memory_space=pl.ANY)
HBM = pl.BlockSpec(memory_space=pltpu.HBM)


def params(mib=16):
    return pltpu.CompilerParams(vmem_limit_bytes=mib * 1024 * 1024)


def normed(block):
    wide = block.astype(F32)
    return (wide * lax.rsqrt(jnp.mean(wide * wide, axis=-1, keepdims=True) + 1e-06)).astype(BF16)


def start_out(
    pair, odd, core, order_ref, band_ref, count_ref, q_ref, k_ref, v_ref, w_ref, t_ref,
    spread_ref, near_ref, cross_ref, pair_out_ref, mine_ref, mask_ref,
    q_in, k_in, v_in, t_in, stage, near, mixed, mine, mask, order, band, count, sems, out_sems,
):
    odd, core = odd[0], core[0]
    depth, slots = w_ref.shape[1], t_ref.shape[2]
    width = w_ref.shape[2] // CHIPS
    loads = [
        (k_ref.at[0], k_in),
        (v_ref.at[0], v_in),
        (q_ref.at[0], q_in),
        (t_ref.at[0], t_in),
    ]
    loads += [
        (w_ref.at[0, :, pl.ds(target * width, width)], stage.at[target, pl.ds(0, depth)])
        for target in range(CHIPS)
    ]
    loads += [(order_ref, order), (band_ref, band), (count_ref, count)]
    loads = [
        pltpu.make_async_copy(source, target, sems.at[i])
        for i, (source, target) in enumerate(loads)
    ]
    for load in loads:
        load.start()
    sent = []

    def send(source, target):
        sent.append(pltpu.make_async_copy(source, target, out_sems.at[len(sent)]))
        sent[-1].start()

    def halves(load, ref, prepare):
        load.wait()
        a, b = prepare(ref[:, :HD]), prepare(ref[:, HD:])
        return jnp.where(odd == 0, a, b), jnp.where(odd == 0, b, a)

    near[0], mixed[0] = halves(loads[0], k_in, normed)
    near[1], mixed[1] = halves(loads[1], v_in, lambda x: x)
    send(near, near_ref)
    send(mixed.at[pl.ds(0, 2)], cross_ref)
    mine[...], mixed[2] = halves(loads[2], q_in, normed)
    send(mixed, pair_out_ref)
    send(mine, mine_ref)
    loads[3].wait()
    for target in range(CHIPS):
        panels = []
        for kind in range(2):
            one, two = (
                jnp.where(odd == 0, t_in[kind, :, at : at + HD], t_in[kind, :, at + HD : at + 2 * HD])
                for at in (4 * target * HD, (4 * target + 2) * HD)
            )
            panels.append((jnp.where(core == 0, one, two), jnp.where(core == 0, two, one)))
        for at, panel in enumerate((panels[0][0], panels[1][0], panels[0][1], panels[1][1])):
            stage[target, depth:, at * HD : (at + 1) * HD] = panel
        stage[target, depth:, 4 * HD :] = jnp.zeros((slots, width - 4 * HD), BF16)
    for load in loads[4 + CHIPS :]:
        load.wait()
    mask[...] = mask_rows(pair[0], odd, core, order, band, count)
    send(mask, mask_ref)
    for target, load in enumerate(loads[4 : 4 + CHIPS]):
        load.wait()
        send(stage.at[target], spread_ref.at[target])
    for copy in sent:
        copy.wait()


def mask_rows(own, odd, core, order, band, count):
    total = order.shape[0] // 4

    def tile_at(pair, slot):
        return order[pair * 4 + ((slot // 2) ^ odd) * 2 + slot % 2]

    lane = lax.broadcasted_iota(jnp.int32, (8, HD), 1)
    row = lax.broadcasted_iota(jnp.int32, (8, HD), 0)
    low = jnp.zeros((8, HD), jnp.int32)
    high = jnp.zeros((8, HD), jnp.int32)
    for slot in range(4):
        tile = tile_at(own, slot)
        low = jnp.where(row == slot, band[0, tile], low)
        high = jnp.where(row == slot, band[1, tile], high)
    held = jnp.full((8, HD), -1, jnp.int32)
    beside = own - 1 + 2 * lax.rem(own, 2)
    for piece, pair in enumerate((own, own ^ 1, own - 2, own + 2, beside)):
        inside = (pair >= 0) & (pair < total)
        kept = jnp.clip(pair, 0, total - 1)
        for slot in range(4):
            tile = jnp.where(inside, tile_at(kept, slot), -1)
            held = jnp.where(lane == 4 * piece + slot, tile, held)
    seen = (held >= low) & (held <= high)
    result = jnp.where((lane <= TEXT_LANE) & jnp.logical_not(seen), F32(FAR), F32(0.0))
    for at, value in ((COUNT_LANE, count[0]), (ODD_LANE, odd), (CORE_LANE, core)):
        result = jnp.where(lane == at, value.astype(F32), result)
    return result


def masked_query(mask_ref, mine_ref, pair_ref):
    query = jnp.concatenate([mine_ref[...], pair_ref[2]], axis=0)
    lane = lax.broadcasted_iota(jnp.int32, (TILE, HD), 1)
    lanes = [
        jnp.where(lane <= TEXT_LANE, mask_ref[slot : slot + 1, :], F32(0.0)).astype(BF16)
        for slot in range(4)
    ]
    return jnp.concatenate([query, jnp.concatenate(lanes, axis=0)], axis=1)


def add_keys(total, query, key, key_lanes, value):
    scores = lax.dot_general(
        query,
        jnp.concatenate([key, key_lanes], axis=1),
        (((1,), (1,)), ((), ())),
        preferred_element_type=F32,
    )
    weights = jnp.exp2(scores * EXP2_SCALE).astype(BF16)
    wide = jnp.concatenate([value, jnp.ones_like(value)], axis=1)
    part = lax.dot_general(weights, wide, (((1,), (0,)), ((), ())), preferred_element_type=F32)
    return part if total is None else total + part


def piece_arrays(index, low_ref, high_ref):
    shape = (PAIR, HD)
    row = lax.broadcasted_iota(jnp.int32, shape, 0)
    lane = lax.broadcasted_iota(jnp.int32, shape, 1)
    lanes = jnp.where(lane == 4 * index + row // TILE, F32(1.0), F32(0.0)).astype(BF16)
    key = jnp.concatenate([low_ref[0], high_ref[0]], axis=0)
    value = jnp.concatenate([low_ref[1], high_ref[1]], axis=0)
    return key, lanes, value


def text_arrays(mask_ref, text_ref, other_core):
    text = text_ref[...]
    chips, held, _ = text.shape
    key = normed(text[:, :, :HD].reshape(chips * held, HD))
    value = text[:, :, HD:].reshape(chips * held, HD)
    row = lax.broadcasted_iota(jnp.int32, key.shape, 0)
    lane = lax.broadcasted_iota(jnp.int32, key.shape, 1)
    core = mask_ref[0:1, CORE_LANE : CORE_LANE + 1]
    side = 1.0 - core if other_core else core
    slot = (2 * (row // held) * held + row % held).astype(F32) + side * held
    dead = (lane == TEXT_LANE) & (slot >= mask_ref[0:1, COUNT_LANE : COUNT_LANE + 1])
    return key, jnp.where(dead, F32(1.0), F32(0.0)).astype(BF16), value


def first_keys(
    mask_ref, mine_ref, near_ref, pair_ref, far_ref, cross_ref, below_ref, above_ref,
    own_text, core_text, total_ref, below, above, sems,
):
    loads = [
        pltpu.make_async_copy(source, target, sems.at[i])
        for i, (source, target) in enumerate(((below_ref, below), (above_ref, above)))
    ]
    for load in loads:
        load.start()
    query = masked_query(mask_ref, mine_ref, pair_ref)
    total = add_keys(None, query, *piece_arrays(0, near_ref, pair_ref))
    total = add_keys(total, query, *piece_arrays(1, far_ref, cross_ref))
    total = add_keys(total, query, *text_arrays(mask_ref, own_text, False))
    total = add_keys(total, query, *text_arrays(mask_ref, core_text, True))
    loads[0].wait()
    total = add_keys(total, query, *piece_arrays(2, below.at[0], below.at[1]))
    loads[1].wait()
    total_ref[...] = add_keys(total, query, *piece_arrays(3, above.at[0], above.at[1]))


def last_keys(mask_ref, mine_ref, pair_ref, sum_ref, beside_ref, out_ref):
    query = masked_query(mask_ref, mine_ref, pair_ref)
    pieces = piece_arrays(PIECES - 1, beside_ref.at[0], beside_ref.at[1])
    total = add_keys(sum_ref[...], query, *pieces)
    result = total[:, :HD] / total[:, HD:]
    odd = mask_ref[0:1, ODD_LANE : ODD_LANE + 1] > 0.5
    own, other = result[:BLOCK], result[BLOCK:]
    to_even = jnp.where(odd, own, other).astype(BF16)
    to_odd = jnp.where(odd, other, own).astype(BF16)
    for chip in range(CHIPS):
        out_ref[chip] = to_even
        out_ref[CHIPS + chip] = to_odd


def join(low_ref, high_ref, out_ref):
    out_ref[0] = low_ref[...]
    out_ref[1] = high_ref[:2]


def project(core, heads_ref, weight_ref, rows_ref, gate_ref, kept_ref, sent_ref):
    total = None
    depth, width = 2 * HD, kept_ref.shape[1]
    for chip in range(CHIPS):
        heads = jnp.concatenate([heads_ref[chip], heads_ref[CHIPS + chip]], axis=1)
        part = jnp.dot(heads, weight_ref[chip, :depth], preferred_element_type=F32)
        total = part if total is None else total + part
    low, high = total[:, :width], total[:, width:]
    first = core[0] == 0
    kept = jnp.where(first, low, high)
    kept_ref[...] = rows_ref[...].astype(F32) + gate_ref[...] * kept
    sent_ref[...] = jnp.where(first, high, low).astype(BF16)


def body(rows, queries, keys, values, text_kv, text_count, out_weight, gate, band, tile_order):
    seq_count = lax.axis_size("seq")
    seq = lax.axis_index("seq")
    grp = lax.axis_index("grp")
    place = [at.astype(jnp.int32).reshape(1) for at in (seq >> 1, seq & 1, grp & 1)]
    shape = jax.ShapeDtypeStruct
    width = gate.shape[1]
    depth, slots = out_weight.shape[1], text_kv.shape[2]

    spread_shape = (CHIPS, depth + slots, 2 * width)
    token_shapes = [(2, BLOCK, HD)] * 2 + [(3, BLOCK, HD), (BLOCK, HD)]
    spread, near, cross_out, pair_out, mine, mask = pl.pallas_call(
        start_out,
        out_shape=[shape(dims, BF16) for dims in [spread_shape, *token_shapes]]
        + [shape((8, HD), F32)],
        in_specs=[SMEM] * 3 + [HBM] * 8,
        out_specs=[HBM] * 6,
        scratch_shapes=[pltpu.VMEM((BLOCK, 2 * HD), BF16)] * 3
        + [pltpu.VMEM(dims, BF16) for dims in [text_kv.shape[1:], spread_shape, *token_shapes[1:]]]
        + [pltpu.VMEM((8, HD), F32)]
        + [pltpu.SMEM(array.shape, jnp.int32) for array in (tile_order, band.T, text_count)]
        + [pltpu.SemaphoreType.DMA(dims) for dims in ((7 + CHIPS,), (5 + CHIPS,))],
        compiler_params=params(60),
        cost_estimate=pl.CostEstimate(flops=10**6, bytes_accessed=4 * 10**6, transcendentals=0),
    )(*place, tile_order, band.T, text_count, queries, keys, values, out_weight, text_kv)

    by_core = [[2 * chip + core for chip in range(CHIPS)] for core in range(2)]
    spread = lax.all_to_all(spread, "grp", 0, 0, axis_index_groups=by_core)

    def swapped(block, mask):
        return lax.ppermute(block, "seq", [(i, i ^ mask) for i in range(seq_count)])

    pair_in = swapped(pair_out, 1)
    far_in = swapped(near, 2)
    cross_in = swapped(cross_out, 3)

    def joined(low, high):
        return pl.pallas_call(
            join,
            out_shape=shape((2, 2, BLOCK, HD), BF16),
            in_specs=[VMEM] * 2,
            compiler_params=params(),
            cost_estimate=pl.CostEstimate(flops=0, bytes_accessed=2**19, transcendentals=0),
        )(low, high)

    own_pair = joined(near, pair_in)
    rows_out, _ = lax.optimization_barrier((rows[0], own_pair))
    after, _ = lax.optimization_barrier((far_in, own_pair))
    rows_in = swapped(rows_out, 1)
    other_pair = joined(after, cross_in)
    up = [(i, i + 4) for i in range(seq_count - 4)]
    down = [(i + 4, i) for i in range(seq_count - 4)]
    below = lax.ppermute(own_pair, "seq", up)
    above = lax.ppermute(own_pair, "seq", down)
    mixed = [(i, j) for i, j in up if i % 4 < 2] + [(i, j) for i, j in down if i % 4 >= 2]
    beside = lax.ppermute(other_pair, "seq", mixed)

    own_text = spread[:, depth:, : 2 * HD]
    core_text = lax.ppermute(
        spread[:, depth:, 2 * HD : 4 * HD], "grp", [(g, g ^ 1) for g in range(2 * CHIPS)]
    )

    def cost(pieces):
        size = 4 * PAIR * pieces * PAIR * 256
        return pl.CostEstimate(flops=size, bytes_accessed=10**6, transcendentals=PAIR * pieces * PAIR)

    total = pl.pallas_call(
        first_keys,
        out_shape=shape((PAIR, 2 * HD), F32),
        in_specs=[VMEM] * 6 + [ANY] * 2 + [VMEM] * 2,
        scratch_shapes=[pltpu.VMEM((2, 2, BLOCK, HD), BF16)] * 2 + [pltpu.SemaphoreType.DMA((2,))],
        compiler_params=params(),
        cost_estimate=cost(5),
    )(mask, mine, near, pair_in, far_in, cross_in, below, above, own_text, core_text)
    total, rows_in = lax.optimization_barrier((total, rows_in))
    attention = pl.pallas_call(
        last_keys,
        out_shape=shape((2 * CHIPS, BLOCK, HD), BF16),
        in_specs=[VMEM] * 5,
        compiler_params=params(),
        cost_estimate=cost(1),
    )(mask, mine, pair_in, total, beside)

    groups = [
        [(2 * pair + odd) * 2 * CHIPS + 2 * chip + core for odd in range(2) for chip in range(CHIPS)]
        for pair in range(seq_count // 2)
        for core in range(2)
    ]
    heads = lax.all_to_all(attention, ("seq", "grp"), 0, 0, axis_index_groups=groups)
    kept, sent = pl.pallas_call(
        project,
        out_shape=(shape((BLOCK, width), F32), shape((BLOCK, width), BF16)),
        in_specs=[SMEM] + [VMEM] * 4,
        compiler_params=params(),
        cost_estimate=pl.CostEstimate(
            flops=2 * BLOCK * 1024 * 768, bytes_accessed=3 * 10**6, transcendentals=0
        ),
    )(place[2], heads, spread, rows_in, gate)
    other = lax.ppermute(sent, "grp", [(g, g ^ 1) for g in range(2 * CHIPS)])
    result = (kept + gate * other.astype(F32)).astype(BF16)
    across = [
        (part * seq_count + i, (1 - part) * seq_count + (i ^ 1))
        for part in range(2)
        for i in range(seq_count)
    ]
    return lax.ppermute(result[None], ("section", "seq"), across)


def solution(mesh):
    placed = (
        P("section", "seq", "grp"),
        P("section", "seq", "grp"),
        P("section", "seq", "grp"),
        P("section", "seq", "grp"),
        P("section", None, "grp", None),
        P("section"),
        P("section", "grp", None),
        P("section", "grp"),
        P(),
        P(),
    )
    return jax.shard_map(
        body, mesh=mesh, in_specs=placed, out_specs=P("section", "seq", "grp"), check_vma=False
    )
```

```python
import math

import jax
import jax.numpy as jnp
from jax import lax
from jax.experimental import pallas as pl
from jax.experimental.pallas import tpu as pltpu
from jax.sharding import PartitionSpec as P

HD = 128
TILE = 128
BLOCK = 256
PAIR = 2 * BLOCK
CHIPS = 4
FAR = -30000.0
EXP2_SCALE = HD ** (-0.5) * math.log2(math.e)
PIECES = 5
TEXT_LANE = 4 * PIECES
COUNT_LANE, ODD_LANE, CORE_LANE = 32, 33, 34
BF16 = jnp.bfloat16
F32 = jnp.float32
SMEM = pl.BlockSpec(memory_space=pltpu.SMEM)
VMEM = pl.BlockSpec(memory_space=pltpu.VMEM)
HBM = pl.BlockSpec(memory_space=pltpu.HBM)


def params(mib=16):
    return pltpu.CompilerParams(vmem_limit_bytes=mib * 1024 * 1024)


def normed(block):
    wide = block.astype(F32)
    return (wide * lax.rsqrt(jnp.mean(wide * wide, axis=-1, keepdims=True) + 1e-06)).astype(BF16)


def start_out(
    pair, odd, core, order_ref, band_ref, count_ref, q_ref, k_ref, v_ref, w_ref, t_ref,
    spread_ref, near_ref, cross_ref, pair_out_ref, mine_ref, mask_ref,
    q_in, k_in, v_in, t_in, stage, near, mixed, mine, mask, order, band, count, sems, out_sems,
):
    odd, core = odd[0], core[0]
    depth, slots = w_ref.shape[1], t_ref.shape[2]
    width = w_ref.shape[2] // CHIPS
    loads = [
        (k_ref.at[0], k_in),
        (v_ref.at[0], v_in),
        (q_ref.at[0], q_in),
        (t_ref.at[0], t_in),
    ]
    loads += [
        (w_ref.at[0, :, pl.ds(target * width, width)], stage.at[target, pl.ds(0, depth)])
        for target in range(CHIPS)
    ]
    loads += [(order_ref, order), (band_ref, band), (count_ref, count)]
    loads = [
        pltpu.make_async_copy(source, target, sems.at[i])
        for i, (source, target) in enumerate(loads)
    ]
    for load in loads:
        load.start()
    sent = []

    def send(source, target):
        sent.append(pltpu.make_async_copy(source, target, out_sems.at[len(sent)]))
        sent[-1].start()

    def halves(load, ref, prepare):
        load.wait()
        a, b = prepare(ref[:, :HD]), prepare(ref[:, HD:])
        return jnp.where(odd == 0, a, b), jnp.where(odd == 0, b, a)

    near[0], mixed[0] = halves(loads[0], k_in, normed)
    near[1], mixed[1] = halves(loads[1], v_in, lambda x: x)
    send(near, near_ref)
    send(mixed.at[pl.ds(0, 2)], cross_ref)
    mine[...], mixed[2] = halves(loads[2], q_in, normed)
    send(mixed, pair_out_ref)
    send(mine, mine_ref)
    loads[3].wait()
    for target in range(CHIPS):
        panels = []
        for kind in range(2):
            one, two = (
                jnp.where(odd == 0, t_in[kind, :, at : at + HD], t_in[kind, :, at + HD : at + 2 * HD])
                for at in (4 * target * HD, (4 * target + 2) * HD)
            )
            panels.append((jnp.where(core == 0, one, two), jnp.where(core == 0, two, one)))
        for at, panel in enumerate((panels[0][0], panels[1][0], panels[0][1], panels[1][1])):
            stage[target, depth:, at * HD : (at + 1) * HD] = panel
        stage[target, depth:, 4 * HD :] = jnp.zeros((slots, width - 4 * HD), BF16)
    for load in loads[4 + CHIPS :]:
        load.wait()
    mask[...] = mask_rows(pair[0], odd, core, order, band, count)
    send(mask, mask_ref)
    for target, load in enumerate(loads[4 : 4 + CHIPS]):
        load.wait()
        send(stage.at[target], spread_ref.at[target])
    for copy in sent:
        copy.wait()


def mask_rows(own, odd, core, order, band, count):
    total = order.shape[0] // 4

    def tile_at(pair, slot):
        return order[pair * 4 + ((slot // 2) ^ odd) * 2 + slot % 2]

    lane = lax.broadcasted_iota(jnp.int32, (8, HD), 1)
    row = lax.broadcasted_iota(jnp.int32, (8, HD), 0)
    low = jnp.zeros((8, HD), jnp.int32)
    high = jnp.zeros((8, HD), jnp.int32)
    for slot in range(4):
        tile = tile_at(own, slot)
        low = jnp.where(row == slot, band[0, tile], low)
        high = jnp.where(row == slot, band[1, tile], high)
    held = jnp.full((8, HD), -1, jnp.int32)
    beside = own - 1 + 2 * lax.rem(own, 2)
    for piece, pair in enumerate((own, own ^ 1, own - 2, own + 2, beside)):
        inside = (pair >= 0) & (pair < total)
        kept = jnp.clip(pair, 0, total - 1)
        for slot in range(4):
            tile = jnp.where(inside, tile_at(kept, slot), -1)
            held = jnp.where(lane == 4 * piece + slot, tile, held)
    seen = (held >= low) & (held <= high)
    result = jnp.where((lane <= TEXT_LANE) & jnp.logical_not(seen), F32(FAR), F32(0.0))
    for at, value in ((COUNT_LANE, count[0]), (ODD_LANE, odd), (CORE_LANE, core)):
        result = jnp.where(lane == at, value.astype(F32), result)
    return result


def masked_query(mask_ref, mine_ref, pair_ref):
    query = jnp.concatenate([mine_ref[...], pair_ref[2]], axis=0)
    lane = lax.broadcasted_iota(jnp.int32, (TILE, HD), 1)
    lanes = [
        jnp.where(lane <= TEXT_LANE, mask_ref[slot : slot + 1, :], F32(0.0)).astype(BF16)
        for slot in range(4)
    ]
    return jnp.concatenate([query, jnp.concatenate(lanes, axis=0)], axis=1)


def add_keys(total, query, key, key_lanes, value):
    scores = lax.dot_general(
        query,
        jnp.concatenate([key, key_lanes], axis=1),
        (((1,), (1,)), ((), ())),
        preferred_element_type=F32,
    )
    weights = jnp.exp2(scores * EXP2_SCALE).astype(BF16)
    wide = jnp.concatenate([value, jnp.ones_like(value)], axis=1)
    part = lax.dot_general(weights, wide, (((1,), (0,)), ((), ())), preferred_element_type=F32)
    return part if total is None else total + part


def piece_arrays(index, low_ref, high_ref):
    shape = (PAIR, HD)
    row = lax.broadcasted_iota(jnp.int32, shape, 0)
    lane = lax.broadcasted_iota(jnp.int32, shape, 1)
    lanes = jnp.where(lane == 4 * index + row // TILE, F32(1.0), F32(0.0)).astype(BF16)
    key = jnp.concatenate([low_ref[0], high_ref[0]], axis=0)
    value = jnp.concatenate([low_ref[1], high_ref[1]], axis=0)
    return key, lanes, value


def text_arrays(mask_ref, text_ref, other_core):
    text = text_ref[...]
    chips, held, _ = text.shape
    key = normed(text[:, :, :HD].reshape(chips * held, HD))
    value = text[:, :, HD:].reshape(chips * held, HD)
    row = lax.broadcasted_iota(jnp.int32, key.shape, 0)
    lane = lax.broadcasted_iota(jnp.int32, key.shape, 1)
    core = mask_ref[0:1, CORE_LANE : CORE_LANE + 1]
    side = 1.0 - core if other_core else core
    slot = (2 * (row // held) * held + row % held).astype(F32) + side * held
    dead = (lane == TEXT_LANE) & (slot >= mask_ref[0:1, COUNT_LANE : COUNT_LANE + 1])
    return key, jnp.where(dead, F32(1.0), F32(0.0)).astype(BF16), value


def first_keys(
    mask_ref, mine_ref, near_ref, pair_ref, far_ref, cross_ref, below_ref, above_ref,
    own_text, core_text, total_ref,
):
    query = masked_query(mask_ref, mine_ref, pair_ref)
    total = add_keys(None, query, *piece_arrays(0, near_ref, pair_ref))
    total = add_keys(total, query, *piece_arrays(1, far_ref, cross_ref))
    total = add_keys(total, query, *text_arrays(mask_ref, own_text, False))
    total = add_keys(total, query, *text_arrays(mask_ref, core_text, True))
    total = add_keys(total, query, *piece_arrays(2, below_ref.at[0], below_ref.at[1]))
    total_ref[...] = add_keys(total, query, *piece_arrays(3, above_ref.at[0], above_ref.at[1]))


def last_keys(mask_ref, mine_ref, pair_ref, sum_ref, beside_ref, out_ref):
    query = masked_query(mask_ref, mine_ref, pair_ref)
    pieces = piece_arrays(PIECES - 1, beside_ref.at[0], beside_ref.at[1])
    total = add_keys(sum_ref[...], query, *pieces)
    result = total[:, :HD] / total[:, HD:]
    odd = mask_ref[0:1, ODD_LANE : ODD_LANE + 1] > 0.5
    own, other = result[:BLOCK], result[BLOCK:]
    to_even = jnp.where(odd, own, other).astype(BF16)
    to_odd = jnp.where(odd, other, own).astype(BF16)
    for chip in range(CHIPS):
        out_ref[chip] = to_even
        out_ref[CHIPS + chip] = to_odd


def join(low_ref, high_ref, out_ref):
    out_ref[0] = low_ref[...]
    out_ref[1] = high_ref[:2]


def project(core, heads_ref, weight_ref, rows_ref, gate_ref, kept_ref, sent_ref):
    total = None
    depth, width = 2 * HD, kept_ref.shape[1]
    for chip in range(CHIPS):
        heads = jnp.concatenate([heads_ref[chip], heads_ref[CHIPS + chip]], axis=1)
        part = jnp.dot(heads, weight_ref[chip, :depth], preferred_element_type=F32)
        total = part if total is None else total + part
    low, high = total[:, :width], total[:, width:]
    first = core[0] == 0
    kept = jnp.where(first, low, high)
    kept_ref[...] = rows_ref[...].astype(F32) + gate_ref[...] * kept
    sent_ref[...] = jnp.where(first, high, low).astype(BF16)


def body(rows, queries, keys, values, text_kv, text_count, out_weight, gate, band, tile_order):
    seq_count = lax.axis_size("seq")
    seq = lax.axis_index("seq")
    grp = lax.axis_index("grp")
    place = [at.astype(jnp.int32).reshape(1) for at in (seq >> 1, seq & 1, grp & 1)]
    shape = jax.ShapeDtypeStruct
    width = gate.shape[1]
    depth, slots = out_weight.shape[1], text_kv.shape[2]

    spread_shape = (CHIPS, depth + slots, 2 * width)
    token_shapes = [(2, BLOCK, HD)] * 2 + [(3, BLOCK, HD), (BLOCK, HD)]
    spread, near, cross_out, pair_out, mine, mask = pl.pallas_call(
        start_out,
        out_shape=[shape(dims, BF16) for dims in [spread_shape, *token_shapes]]
        + [shape((8, HD), F32)],
        in_specs=[SMEM] * 3 + [HBM] * 8,
        out_specs=[HBM] * 6,
        scratch_shapes=[pltpu.VMEM((BLOCK, 2 * HD), BF16)] * 3
        + [pltpu.VMEM(dims, BF16) for dims in [text_kv.shape[1:], spread_shape, *token_shapes[1:]]]
        + [pltpu.VMEM((8, HD), F32)]
        + [pltpu.SMEM(array.shape, jnp.int32) for array in (tile_order, band.T, text_count)]
        + [pltpu.SemaphoreType.DMA(dims) for dims in ((7 + CHIPS,), (5 + CHIPS,))],
        compiler_params=params(60),
        cost_estimate=pl.CostEstimate(flops=10**6, bytes_accessed=4 * 10**6, transcendentals=0),
    )(*place, tile_order, band.T, text_count, queries, keys, values, out_weight, text_kv)

    by_core = [[2 * chip + core for chip in range(CHIPS)] for core in range(2)]
    spread = lax.all_to_all(spread, "grp", 0, 0, axis_index_groups=by_core)

    def swapped(block, mask):
        return lax.ppermute(block, "seq", [(i, i ^ mask) for i in range(seq_count)])

    pair_in = swapped(pair_out, 1)
    far_in = swapped(near, 2)
    cross_in = swapped(cross_out, 3)

    def joined(low, high):
        return pl.pallas_call(
            join,
            out_shape=shape((2, 2, BLOCK, HD), BF16),
            in_specs=[VMEM] * 2,
            compiler_params=params(),
            cost_estimate=pl.CostEstimate(flops=0, bytes_accessed=2**19, transcendentals=0),
        )(low, high)

    pair_in, rows_out = lax.optimization_barrier((pair_in, rows[0]))
    own_pair = joined(near, pair_in)
    rows_in = swapped(rows_out, 1)
    after, _ = lax.optimization_barrier((far_in, own_pair))
    other_pair = joined(after, cross_in)
    up = [(i, i + 4) for i in range(seq_count - 4)]
    down = [(i + 4, i) for i in range(seq_count - 4)]
    below = lax.ppermute(own_pair, "seq", up)
    above = lax.ppermute(own_pair, "seq", down)
    mixed = [(i, j) for i, j in up if i % 4 < 2] + [(i, j) for i, j in down if i % 4 >= 2]
    beside = lax.ppermute(other_pair, "seq", mixed)

    own_text = spread[:, depth:, : 2 * HD]
    core_text = lax.ppermute(
        spread[:, depth:, 2 * HD : 4 * HD], "grp", [(g, g ^ 1) for g in range(2 * CHIPS)]
    )

    def cost(pieces):
        size = 4 * PAIR * pieces * PAIR * 256
        return pl.CostEstimate(flops=size, bytes_accessed=10**6, transcendentals=PAIR * pieces * PAIR)

    mask, rows_in = lax.optimization_barrier((mask, rows_in))
    total = pl.pallas_call(
        first_keys,
        out_shape=shape((PAIR, 2 * HD), F32),
        in_specs=[VMEM] * 10,
        compiler_params=params(),
        cost_estimate=cost(5),
    )(mask, mine, near, pair_in, far_in, cross_in, below, above, own_text, core_text)
    attention = pl.pallas_call(
        last_keys,
        out_shape=shape((2 * CHIPS, BLOCK, HD), BF16),
        in_specs=[VMEM] * 5,
        compiler_params=params(),
        cost_estimate=cost(1),
    )(mask, mine, pair_in, total, beside)

    groups = [
        [(2 * pair + odd) * 2 * CHIPS + 2 * chip + core for odd in range(2) for chip in range(CHIPS)]
        for pair in range(seq_count // 2)
        for core in range(2)
    ]
    heads = lax.all_to_all(attention, ("seq", "grp"), 0, 0, axis_index_groups=groups)
    kept, sent = pl.pallas_call(
        project,
        out_shape=(shape((BLOCK, width), F32), shape((BLOCK, width), BF16)),
        in_specs=[SMEM] + [VMEM] * 4,
        compiler_params=params(),
        cost_estimate=pl.CostEstimate(
            flops=2 * BLOCK * 1024 * 768, bytes_accessed=3 * 10**6, transcendentals=0
        ),
    )(place[2], heads, spread, rows_in, gate)
    other = lax.ppermute(sent, "grp", [(g, g ^ 1) for g in range(2 * CHIPS)])
    result = (kept + gate * other.astype(F32)).astype(BF16)
    across = [
        (part * seq_count + i, (1 - part) * seq_count + (i ^ 1))
        for part in range(2)
        for i in range(seq_count)
    ]
    return lax.ppermute(result[None], ("section", "seq"), across)


def solution(mesh):
    placed = (
        P("section", "seq", "grp"),
        P("section", "seq", "grp"),
        P("section", "seq", "grp"),
        P("section", "seq", "grp"),
        P("section", None, "grp", None),
        P("section"),
        P("section", "grp", None),
        P("section", "grp"),
        P(),
        P(),
    )
    return jax.shard_map(
        body, mesh=mesh, in_specs=placed, out_specs=P("section", "seq", "grp"), check_vma=False
    )
```

```python
import math

import jax
import jax.numpy as jnp
from jax import lax
from jax.experimental import pallas as pl
from jax.experimental.pallas import tpu as pltpu
from jax.sharding import PartitionSpec as P

HD = 128
TILE = 128
BLOCK = 256
PAIR = 2 * BLOCK
CHIPS = 4
FAR = -30000.0
EXP2_SCALE = HD ** (-0.5) * math.log2(math.e)
PIECES = 5
TEXT_LANE = 4 * PIECES
ODD_LANE, CORE_LANE = 32, 33
BF16 = jnp.bfloat16
F32 = jnp.float32
SMEM = pl.BlockSpec(memory_space=pltpu.SMEM)
VMEM = pl.BlockSpec(memory_space=pltpu.VMEM)
HBM = pl.BlockSpec(memory_space=pltpu.HBM)


def params(mib=16):
    return pltpu.CompilerParams(vmem_limit_bytes=mib * 1024 * 1024)


def normed(block):
    wide = block.astype(F32)
    return (wide * lax.rsqrt(jnp.mean(wide * wide, axis=-1, keepdims=True) + 1e-06)).astype(BF16)


def start_out(
    pair, odd, core, order_ref, band_ref, q_ref, k_ref, v_ref, w_ref, t_ref,
    spread_ref, near_ref, cross_ref, pair_out_ref, mine_ref, mask_ref,
    q_in, k_in, v_in, t_in, order, band, sems,
):
    odd, core = odd[0], core[0]
    depth, slots = w_ref.shape[1], t_ref.shape[2]
    width = w_ref.shape[2] // CHIPS
    loads = [
        (k_ref.at[0], k_in),
        (v_ref.at[0], v_in),
        (q_ref.at[0], q_in),
        (t_ref.at[0], t_in),
        (order_ref, order),
        (band_ref, band),
    ]
    loads += [
        (w_ref.at[0, :, pl.ds(target * width, width)], spread_ref.at[target, pl.ds(0, depth)])
        for target in range(CHIPS)
    ]
    loads = [
        pltpu.make_async_copy(source, target, sems.at[i])
        for i, (source, target) in enumerate(loads)
    ]
    for load in loads:
        load.start()

    def halves(load, ref, prepare):
        load.wait()
        a, b = prepare(ref[:, :HD]), prepare(ref[:, HD:])
        return jnp.where(odd == 0, a, b), jnp.where(odd == 0, b, a)

    near_ref[0], key_other = halves(loads[0], k_in, normed)
    near_ref[1], value_other = halves(loads[1], v_in, lambda x: x)
    mine_ref[...], pair_out_ref[2] = halves(loads[2], q_in, normed)
    for ref in (cross_ref, pair_out_ref):
        ref[0] = key_other
        ref[1] = value_other
    loads[3].wait()
    for target in range(CHIPS):
        panels = []
        for kind in range(2):
            one, two = (
                jnp.where(odd == 0, t_in[kind, :, at : at + HD], t_in[kind, :, at + HD : at + 2 * HD])
                for at in (4 * target * HD, (4 * target + 2) * HD)
            )
            panels.append((jnp.where(core == 0, one, two), jnp.where(core == 0, two, one)))
        for at, panel in enumerate((panels[0][0], panels[1][0], panels[0][1], panels[1][1])):
            spread_ref[target, depth:, at * HD : (at + 1) * HD] = panel
        spread_ref[target, depth:, 4 * HD :] = jnp.zeros((slots, width - 4 * HD), BF16)
    for load in loads[4:6]:
        load.wait()
    mask_ref[...] = mask_rows(pair[0], odd, core, order, band)
    for load in loads[6:]:
        load.wait()


def mask_rows(own, odd, core, order, band):
    total = order.shape[0] // 4

    def tile_at(pair, slot):
        return order[pair * 4 + ((slot // 2) ^ odd) * 2 + slot % 2]

    lane = lax.broadcasted_iota(jnp.int32, (8, HD), 1)
    row = lax.broadcasted_iota(jnp.int32, (8, HD), 0)
    low = jnp.zeros((8, HD), jnp.int32)
    high = jnp.zeros((8, HD), jnp.int32)
    for slot in range(4):
        tile = tile_at(own, slot)
        low = jnp.where(row == slot, band[0, tile], low)
        high = jnp.where(row == slot, band[1, tile], high)
    held = jnp.full((8, HD), -1, jnp.int32)
    beside = own - 1 + 2 * lax.rem(own, 2)
    for piece, pair in enumerate((own, own ^ 1, own - 2, own + 2, beside)):
        inside = (pair >= 0) & (pair < total)
        kept = jnp.clip(pair, 0, total - 1)
        for slot in range(4):
            tile = jnp.where(inside, tile_at(kept, slot), -1)
            held = jnp.where(lane == 4 * piece + slot, tile, held)
    seen = (held >= low) & (held <= high)
    result = jnp.where((lane <= TEXT_LANE) & jnp.logical_not(seen), F32(FAR), F32(0.0))
    for at, value in ((ODD_LANE, odd), (CORE_LANE, core)):
        result = jnp.where(lane == at, value.astype(F32), result)
    return result


def masked_query(mask_ref, mine_ref, pair_ref):
    query = jnp.concatenate([mine_ref[...], pair_ref[2]], axis=0)
    lane = lax.broadcasted_iota(jnp.int32, (TILE, HD), 1)
    lanes = [
        jnp.where(lane <= TEXT_LANE, mask_ref[slot : slot + 1, :], F32(0.0)).astype(BF16)
        for slot in range(4)
    ]
    return jnp.concatenate([query, jnp.concatenate(lanes, axis=0)], axis=1)


def add_keys(total, query, key, key_lanes, value):
    scores = lax.dot_general(
        query,
        jnp.concatenate([key, key_lanes], axis=1),
        (((1,), (1,)), ((), ())),
        preferred_element_type=F32,
    )
    weights = jnp.exp2(scores * EXP2_SCALE).astype(BF16)
    wide = jnp.concatenate([value, jnp.ones_like(value)], axis=1)
    part = lax.dot_general(weights, wide, (((1,), (0,)), ((), ())), preferred_element_type=F32)
    return part if total is None else total + part


def piece_arrays(index, low_ref, high_ref):
    shape = (PAIR, HD)
    row = lax.broadcasted_iota(jnp.int32, shape, 0)
    lane = lax.broadcasted_iota(jnp.int32, shape, 1)
    lanes = jnp.where(lane == 4 * index + row // TILE, F32(1.0), F32(0.0)).astype(BF16)
    key = jnp.concatenate([low_ref[0], high_ref[0]], axis=0)
    value = jnp.concatenate([low_ref[1], high_ref[1]], axis=0)
    return key, lanes, value


def text_arrays(count, mask_ref, text_ref, other_core):
    text = text_ref[...]
    chips, held, _ = text.shape
    key = normed(text[:, :, :HD].reshape(chips * held, HD))
    value = text[:, :, HD:].reshape(chips * held, HD)
    row = lax.broadcasted_iota(jnp.int32, key.shape, 0)
    lane = lax.broadcasted_iota(jnp.int32, key.shape, 1)
    core = mask_ref[0:1, CORE_LANE : CORE_LANE + 1]
    side = 1.0 - core if other_core else core
    slot = (2 * (row // held) * held + row % held).astype(F32) + side * held
    dead = (lane == TEXT_LANE) & (slot >= count[0].astype(F32))
    return key, jnp.where(dead, F32(1.0), F32(0.0)).astype(BF16), value


def first_keys(
    mask_ref, mine_ref, near_ref, pair_ref, far_ref, cross_ref, below_ref, above_ref, total_ref
):
    query = masked_query(mask_ref, mine_ref, pair_ref)
    total = add_keys(None, query, *piece_arrays(0, near_ref, pair_ref))
    total = add_keys(total, query, *piece_arrays(1, far_ref, cross_ref))
    total = add_keys(total, query, *piece_arrays(2, below_ref.at[0], below_ref.at[1]))
    total_ref[...] = add_keys(total, query, *piece_arrays(3, above_ref.at[0], above_ref.at[1]))


def last_keys(
    count, mask_ref, mine_ref, pair_ref, sum_ref, own_text, core_text, beside_ref, out_ref
):
    query = masked_query(mask_ref, mine_ref, pair_ref)
    texts = zip(
        text_arrays(count, mask_ref, own_text, False), text_arrays(count, mask_ref, core_text, True)
    )
    total = add_keys(sum_ref[...], query, *(jnp.concatenate(both, axis=0) for both in texts))
    pieces = piece_arrays(PIECES - 1, beside_ref.at[0], beside_ref.at[1])
    total = add_keys(total, query, *pieces)
    result = total[:, :HD] / total[:, HD:]
    odd = mask_ref[0:1, ODD_LANE : ODD_LANE + 1] > 0.5
    own, other = result[:BLOCK], result[BLOCK:]
    to_even = jnp.where(odd, own, other).astype(BF16)
    to_odd = jnp.where(odd, other, own).astype(BF16)
    for chip in range(CHIPS):
        out_ref[chip] = to_even
        out_ref[CHIPS + chip] = to_odd


def join(low_ref, high_ref, out_ref):
    out_ref[0] = low_ref[...]
    out_ref[1] = high_ref[:2]


def project(core, heads_ref, weight_ref, rows_ref, gate_ref, kept_ref, sent_ref):
    total = None
    depth, width = 2 * HD, kept_ref.shape[1]
    for chip in range(CHIPS):
        heads = jnp.concatenate([heads_ref[chip], heads_ref[CHIPS + chip]], axis=1)
        part = jnp.dot(heads, weight_ref[chip, :depth], preferred_element_type=F32)
        total = part if total is None else total + part
    low, high = total[:, :width], total[:, width:]
    first = core[0] == 0
    kept = jnp.where(first, low, high)
    kept_ref[...] = rows_ref[...].astype(F32) + gate_ref[...] * kept
    sent_ref[...] = jnp.where(first, high, low).astype(BF16)


def body(rows, queries, keys, values, text_kv, text_count, out_weight, gate, band, tile_order):
    seq_count = lax.axis_size("seq")
    seq = lax.axis_index("seq")
    grp = lax.axis_index("grp")
    place = [at.astype(jnp.int32).reshape(1) for at in (seq >> 1, seq & 1, grp & 1)]
    shape = jax.ShapeDtypeStruct
    width = gate.shape[1]
    depth, slots = out_weight.shape[1], text_kv.shape[2]

    spread_shape = (CHIPS, depth + slots, 2 * width)
    token_shapes = [(2, BLOCK, HD)] * 2 + [(3, BLOCK, HD), (BLOCK, HD)]
    loaded = (tile_order, band.T, queries, keys, values, out_weight, text_kv)
    spread, near, cross_out, pair_out, mine, mask = pl.pallas_call(
        start_out,
        out_shape=[pltpu.VMEM(dims, BF16) for dims in [spread_shape, *token_shapes]]
        + [pltpu.VMEM((8, HD), F32)],
        in_specs=[SMEM] * 3 + [HBM] * 7,
        out_specs=[VMEM] * 6,
        scratch_shapes=[pltpu.VMEM((BLOCK, 2 * HD), BF16)] * 3
        + [pltpu.VMEM(text_kv.shape[1:], BF16)]
        + [pltpu.SMEM(array.shape, jnp.int32) for array in loaded[:2]]
        + [pltpu.SemaphoreType.DMA((6 + CHIPS,))],
        compiler_params=params(),
        cost_estimate=pl.CostEstimate(flops=10**6, bytes_accessed=4 * 10**6, transcendentals=0),
    )(*place, *(pltpu.with_memory_space_constraint(a, pltpu.HBM) for a in loaded))

    by_core = [[2 * chip + core for chip in range(CHIPS)] for core in range(2)]
    spread = lax.all_to_all(spread, "grp", 0, 0, axis_index_groups=by_core)

    def swapped(block, mask):
        return lax.ppermute(block, "seq", [(i, i ^ mask) for i in range(seq_count)])

    pair_in = swapped(pair_out, 1)
    far_in = swapped(near, 2)
    cross_in = swapped(cross_out, 3)

    def joined(low, high):
        return pl.pallas_call(
            join,
            out_shape=shape((2, 2, BLOCK, HD), BF16),
            in_specs=[VMEM] * 2,
            compiler_params=params(),
            cost_estimate=pl.CostEstimate(flops=0, bytes_accessed=2**19, transcendentals=0),
        )(low, high)

    pair_in, rows_out = lax.optimization_barrier((pair_in, rows[0]))
    own_pair = joined(near, pair_in)
    rows_in = swapped(rows_out, 1)
    after, _ = lax.optimization_barrier((far_in, own_pair))
    other_pair = joined(after, cross_in)
    up = [(i, i + 4) for i in range(seq_count - 4)]
    down = [(i + 4, i) for i in range(seq_count - 4)]
    below = lax.ppermute(own_pair, "seq", up)
    above = lax.ppermute(own_pair, "seq", down)
    mixed = [(i, j) for i, j in up if i % 4 < 2] + [(i, j) for i, j in down if i % 4 >= 2]
    beside = lax.ppermute(other_pair, "seq", mixed)

    own_text = spread[:, depth:, : 2 * HD]
    core_text = lax.ppermute(
        spread[:, depth:, 2 * HD : 4 * HD], "grp", [(g, g ^ 1) for g in range(2 * CHIPS)]
    )

    def cost(pieces):
        size = 4 * PAIR * pieces * PAIR * 256
        return pl.CostEstimate(flops=size, bytes_accessed=10**6, transcendentals=PAIR * pieces * PAIR)

    total = pl.pallas_call(
        first_keys,
        out_shape=shape((PAIR, 2 * HD), F32),
        in_specs=[VMEM] * 8,
        compiler_params=params(),
        cost_estimate=cost(5),
    )(mask, mine, near, pair_in, far_in, cross_in, below, above)
    total, rows_in = lax.optimization_barrier((total, rows_in))
    attention = pl.pallas_call(
        last_keys,
        out_shape=shape((2 * CHIPS, BLOCK, HD), BF16),
        in_specs=[SMEM] + [VMEM] * 7,
        compiler_params=params(),
        cost_estimate=cost(1),
    )(text_count, mask, mine, pair_in, total, own_text, core_text, beside)

    groups = [
        [(2 * pair + odd) * 2 * CHIPS + 2 * chip + core for odd in range(2) for chip in range(CHIPS)]
        for pair in range(seq_count // 2)
        for core in range(2)
    ]
    heads = lax.all_to_all(attention, ("seq", "grp"), 0, 0, axis_index_groups=groups)
    kept, sent = pl.pallas_call(
        project,
        out_shape=(shape((BLOCK, width), F32), shape((BLOCK, width), BF16)),
        in_specs=[SMEM] + [VMEM] * 4,
        compiler_params=params(),
        cost_estimate=pl.CostEstimate(
            flops=2 * BLOCK * 1024 * 768, bytes_accessed=3 * 10**6, transcendentals=0
        ),
    )(place[2], heads, spread, rows_in, gate)
    other = lax.ppermute(sent, "grp", [(g, g ^ 1) for g in range(2 * CHIPS)])
    result = (kept + gate * other.astype(F32)).astype(BF16)
    across = [
        (part * seq_count + i, (1 - part) * seq_count + (i ^ 1))
        for part in range(2)
        for i in range(seq_count)
    ]
    return lax.ppermute(result[None], ("section", "seq"), across)


def solution(mesh):
    placed = (
        P("section", "seq", "grp"),
        P("section", "seq", "grp"),
        P("section", "seq", "grp"),
        P("section", "seq", "grp"),
        P("section", None, "grp", None),
        P("section"),
        P("section", "grp", None),
        P("section", "grp"),
        P(),
        P(),
    )
    return jax.shard_map(
        body, mesh=mesh, in_specs=placed, out_specs=P("section", "seq", "grp"), check_vma=False
    )
```

```python
import math

import jax
import jax.numpy as jnp
from jax import lax
from jax.experimental import pallas as pl
from jax.experimental.pallas import tpu as pltpu
from jax.sharding import PartitionSpec as P

HD = 128
TILE = 128
BLOCK = 256
PAIR = 2 * BLOCK
CHIPS = 4
FAR = -30000.0
EXP2_SCALE = HD ** (-0.5) * math.log2(math.e)
PIECES = 5
TEXT_LANE = 4 * PIECES
ODD_LANE = 32

BF16 = jnp.bfloat16
F32 = jnp.float32
SMEM = pl.BlockSpec(memory_space=pltpu.SMEM)
VMEM = pl.BlockSpec(memory_space=pltpu.VMEM)
HBM = pl.BlockSpec(memory_space=pltpu.HBM)


def params(mib=16):
    return pltpu.CompilerParams(vmem_limit_bytes=mib * 1024 * 1024)


def normed(block):
    wide = block.astype(F32)
    return (wide * lax.rsqrt(jnp.mean(wide * wide, axis=-1, keepdims=True) + 1e-06)).astype(BF16)


def start_out(
    pair, odd, order_ref, band_ref, q_ref, k_ref, v_ref, r_ref, w_ref, t_ref,
    spread_ref, near_ref, cross_ref, along_ref, mine_ref, rows_ref, mask_ref,
    q_in, k_in, v_in, t_in, order, band, sems,
):
    odd = odd[0]
    depth, slots = w_ref.shape[1], t_ref.shape[2]
    targets, width = spread_ref.shape[0], spread_ref.shape[2]
    loads = [
        (k_ref.at[0], k_in),
        (v_ref.at[0], v_in),
        (q_ref.at[0], q_in),
        (t_ref.at[0], t_in),
        (order_ref, order),
        (band_ref, band),
        (r_ref.at[0], rows_ref),
    ]
    loads += [
        (w_ref.at[0, :, pl.ds(target * width, width)], spread_ref.at[target, pl.ds(0, depth)])
        for target in range(targets)
    ]
    loads = [
        pltpu.make_async_copy(source, target, sems.at[i])
        for i, (source, target) in enumerate(loads)
    ]
    for load in loads:
        load.start()

    def own_first(a, b):
        return jnp.where(odd == 0, a, b), jnp.where(odd == 0, b, a)

    def halves(load, ref, prepare):
        load.wait()
        return own_first(prepare(ref[:, :HD]), prepare(ref[:, HD:]))

    near_ref[0], key_other = halves(loads[0], k_in, normed)
    near_ref[1], value_other = halves(loads[1], v_in, lambda x: x)
    mine_ref[...], query_other = halves(loads[2], q_in, normed)
    cross_ref[0] = key_other
    cross_ref[1] = value_other
    for at, block in enumerate((key_other, value_other, query_other)):
        along_ref[:, at * HD : (at + 1) * HD] = block
    loads[3].wait()
    for target in range(targets):
        at = 2 * target * HD
        for kind in range(2):
            panel, _ = own_first(t_in[kind, :, at : at + HD], t_in[kind, :, at + HD : at + 2 * HD])
            spread_ref[target, depth:, kind * HD : (kind + 1) * HD] = panel
        spread_ref[target, depth:, 2 * HD :] = jnp.zeros((slots, width - 2 * HD), BF16)
    for load in loads[4:6]:
        load.wait()
    mask_ref[...] = mask_rows(pair[0], odd, order, band)
    for load in loads[6:]:
        load.wait()


def mask_rows(own, odd, order, band):
    total = order.shape[0] // 4

    def tile_at(pair, slot):
        return order[pair * 4 + ((slot // 2) ^ odd) * 2 + slot % 2]

    lane = lax.broadcasted_iota(jnp.int32, (8, HD), 1)
    row = lax.broadcasted_iota(jnp.int32, (8, HD), 0)
    low = jnp.zeros((8, HD), jnp.int32)
    high = jnp.zeros((8, HD), jnp.int32)
    for slot in range(4):
        tile = tile_at(own, slot)
        low = jnp.where(row == slot, band[0, tile], low)
        high = jnp.where(row == slot, band[1, tile], high)
    held = jnp.full((8, HD), -1, jnp.int32)
    beside = own - 1 + 2 * lax.rem(own, 2)
    for piece, pair in enumerate((own, own ^ 1, own - 2, own + 2, beside)):
        inside = (pair >= 0) & (pair < total)
        kept = jnp.clip(pair, 0, total - 1)
        for slot in range(4):
            tile = jnp.where(inside, tile_at(kept, slot), -1)
            held = jnp.where(lane == 4 * piece + slot, tile, held)
    seen = (held >= low) & (held <= high)
    result = jnp.where((lane <= TEXT_LANE) & jnp.logical_not(seen), F32(FAR), F32(0.0))
    return jnp.where(lane == ODD_LANE, odd.astype(F32), result)


def masked_query(mask_ref, mine_ref, along_ref):
    query = jnp.concatenate([mine_ref[...], along_ref[:, 2 * HD : 3 * HD]], axis=0)
    lane = lax.broadcasted_iota(jnp.int32, (TILE, HD), 1)
    lanes = [
        jnp.where(lane <= TEXT_LANE, mask_ref[slot : slot + 1, :], F32(0.0)).astype(BF16)
        for slot in range(4)
    ]
    return jnp.concatenate([query, jnp.concatenate(lanes, axis=0)], axis=1)


def add_keys(total, query, key, key_lanes, value):
    scores = lax.dot_general(
        query,
        jnp.concatenate([key, key_lanes], axis=1),
        (((1,), (1,)), ((), ())),
        preferred_element_type=F32,
    )
    weights = jnp.exp2(scores * EXP2_SCALE).astype(BF16)
    wide = jnp.concatenate([value, jnp.ones_like(value)], axis=1)
    part = lax.dot_general(weights, wide, (((1,), (0,)), ((), ())), preferred_element_type=F32)
    return part if total is None else total + part


def piece_arrays(index, low_ref, high_ref):
    shape = (PAIR, HD)
    row = lax.broadcasted_iota(jnp.int32, shape, 0)
    lane = lax.broadcasted_iota(jnp.int32, shape, 1)
    lanes = jnp.where(lane == 4 * index + row // TILE, F32(1.0), F32(0.0)).astype(BF16)
    key = jnp.concatenate([low_ref[0], high_ref[0]], axis=0)
    value = jnp.concatenate([low_ref[1], high_ref[1]], axis=0)
    return key, lanes, value


def text_arrays(count, text_ref):
    groups, held, _ = text_ref.shape
    text = text_ref[...].reshape(groups * held, 2 * HD)
    shape = (groups * held, HD)
    slot = lax.broadcasted_iota(jnp.int32, shape, 0)
    lane = lax.broadcasted_iota(jnp.int32, shape, 1)
    dead = jnp.where((lane == TEXT_LANE) & (slot >= count[0]), F32(1.0), F32(0.0))
    return normed(text[:, :HD]), dead.astype(BF16), text[:, HD:]


def first_keys(
    mask_ref, mine_ref, along_ref, own_ref, other_ref, below_ref, above_ref, total_ref
):
    query = masked_query(mask_ref, mine_ref, along_ref)
    total = None
    for piece, ref in enumerate((own_ref, other_ref, below_ref, above_ref)):
        total = add_keys(total, query, *piece_arrays(piece, ref.at[0], ref.at[1]))
    total_ref[...] = total


def last_keys(count, mask_ref, mine_ref, along_ref, sum_ref, text_ref, beside_ref, out_ref):
    query = masked_query(mask_ref, mine_ref, along_ref)
    total = add_keys(sum_ref[...], query, *text_arrays(count, text_ref))
    pieces = piece_arrays(PIECES - 1, beside_ref.at[0], beside_ref.at[1])
    total = add_keys(total, query, *pieces)
    result = total[:, :HD] / total[:, HD:]
    odd = mask_ref[0:1, ODD_LANE : ODD_LANE + 1] > 0.5
    own, other = result[:BLOCK], result[BLOCK:]
    to_even = jnp.where(odd, own, other).astype(BF16)
    to_odd = jnp.where(odd, other, own).astype(BF16)
    for chip in range(CHIPS):
        out_ref[chip] = to_even
        out_ref[CHIPS + chip] = to_odd


def join(low_ref, high_ref, out_ref):
    out_ref[0] = low_ref[...]
    out_ref[1] = high_ref[...]


def join_pair(low_ref, along_ref, out_ref):
    out_ref[0] = low_ref[...]
    for kind in range(2):
        out_ref[1, kind] = along_ref[:, kind * HD : (kind + 1) * HD]


def projected(core, heads_ref, weight_ref):
    total = None
    for chip in range(CHIPS):
        heads = jnp.concatenate([heads_ref[chip], heads_ref[CHIPS + chip]], axis=1)
        weight = weight_ref[2 * chip + core, : 2 * HD]
        part = jnp.dot(heads, weight, preferred_element_type=F32)
        total = part if total is None else total + part
    return total


def project_own(core, heads_ref, weight_ref, kept_ref):
    kept_ref[...] = projected(core[0], heads_ref, weight_ref)


def project_other(core, heads_ref, weight_ref, kept_ref, rows_ref, gate_ref, out_ref):
    share = kept_ref[...] + projected(1 - core[0], heads_ref, weight_ref)
    rows = rows_ref[...].astype(F32)
    out_ref[...] = (rows + gate_ref[...] * share).astype(BF16)


def body(rows, queries, keys, values, text_kv, text_count, out_weight, gate, band, tile_order):
    seq_count = lax.axis_size("seq")
    seq = lax.axis_index("seq")
    grp = lax.axis_index("grp")
    place = [at.astype(jnp.int32).reshape(1) for at in (seq >> 1, seq & 1, grp & 1)]
    shape = jax.ShapeDtypeStruct
    width = gate.shape[1]
    depth, slots = out_weight.shape[1], text_kv.shape[2]

    spread_shape = (2 * CHIPS, depth + slots, width)
    token_shapes = [(2, BLOCK, HD)] * 2 + [(BLOCK, 3 * HD), (BLOCK, HD), (BLOCK, width)]
    loaded = (tile_order, band.T, queries, keys, values, rows, out_weight, text_kv)
    spread, near, cross_out, along, mine, rows_out, mask = pl.pallas_call(
        start_out,
        out_shape=[pltpu.VMEM(dims, BF16) for dims in [spread_shape, *token_shapes]]
        + [pltpu.VMEM((8, HD), F32)],
        in_specs=[SMEM] * 2 + [HBM] * 8,
        out_specs=[VMEM] * 7,
        scratch_shapes=[pltpu.VMEM((BLOCK, 2 * HD), BF16)] * 3
        + [pltpu.VMEM(text_kv.shape[1:], BF16)]
        + [pltpu.SMEM(array.shape, jnp.int32) for array in loaded[:2]]
        + [pltpu.SemaphoreType.DMA((7 + 2 * CHIPS,))],
        compiler_params=params(),
        cost_estimate=pl.CostEstimate(flops=10**6, bytes_accessed=4 * 10**6, transcendentals=0),
    )(*place[:2], *(pltpu.with_memory_space_constraint(a, pltpu.HBM) for a in loaded))

    spread = lax.all_to_all(spread, "grp", 0, 0)

    def swapped(block, mask):
        return lax.ppermute(block, "seq", [(i, i ^ mask) for i in range(seq_count)])

    along_in = swapped(along, 1)
    far_in = swapped(near, 2)
    cross_in = swapped(cross_out, 3)

    def joined(kernel, low, high):
        return pl.pallas_call(
            kernel,
            out_shape=shape((2, 2, BLOCK, HD), BF16),
            in_specs=[VMEM] * 2,
            compiler_params=params(),
            cost_estimate=pl.CostEstimate(flops=0, bytes_accessed=2**19, transcendentals=0),
        )(low, high)

    along_in, rows_out = lax.optimization_barrier((along_in, rows_out))
    own_pair = joined(join_pair, near, along_in)
    rows_in = swapped(rows_out, 1)
    after, _ = lax.optimization_barrier((far_in, own_pair))
    other_pair = joined(join, after, cross_in)
    up = [(i, i + 4) for i in range(seq_count - 4)]
    down = [(i + 4, i) for i in range(seq_count - 4)]
    below = lax.ppermute(own_pair, "seq", up)
    above = lax.ppermute(own_pair, "seq", down)
    mixed = [(i, j) for i, j in up if i % 4 < 2] + [(i, j) for i, j in down if i % 4 >= 2]
    beside = lax.ppermute(other_pair, "seq", mixed)
    text = spread[:, depth:, : 2 * HD]

    def cost(pieces):
        size = 4 * PAIR * pieces * PAIR * 256
        return pl.CostEstimate(flops=size, bytes_accessed=10**6, transcendentals=PAIR * pieces * PAIR)

    mask, rows_in = lax.optimization_barrier((mask, rows_in))
    total = pl.pallas_call(
        first_keys,
        out_shape=shape((PAIR, 2 * HD), F32),
        in_specs=[VMEM] * 7,
        compiler_params=params(),
        cost_estimate=cost(5),
    )(mask, mine, along_in, own_pair, other_pair, below, above)
    attention = pl.pallas_call(
        last_keys,
        out_shape=shape((2 * CHIPS, BLOCK, HD), BF16),
        in_specs=[SMEM] + [VMEM] * 6,
        compiler_params=params(),
        cost_estimate=cost(1),
    )(text_count, mask, mine, along_in, total, text, beside)

    groups = [
        [(2 * pair + odd) * 2 * CHIPS + 2 * chip + core for odd in range(2) for chip in range(CHIPS)]
        for pair in range(seq_count // 2)
        for core in range(2)
    ]
    heads = lax.all_to_all(attention, ("seq", "grp"), 0, 0, axis_index_groups=groups)
    other_heads = lax.ppermute(heads, "grp", [(g, g ^ 1) for g in range(2 * CHIPS)])
    half = pl.CostEstimate(flops=2 * BLOCK * 1024 * 384, bytes_accessed=10**6, transcendentals=0)
    kept = pl.pallas_call(
        project_own,
        out_shape=shape((BLOCK, width), F32),
        in_specs=[SMEM] + [VMEM] * 2,
        compiler_params=params(),
        cost_estimate=half,
    )(place[2], heads, spread)
    result = pl.pallas_call(
        project_other,
        out_shape=shape((BLOCK, width), BF16),
        in_specs=[SMEM] + [VMEM] * 5,
        compiler_params=params(),
        cost_estimate=half,
    )(place[2], other_heads, spread, kept, rows_in, gate)
    across = [
        (part * seq_count + i, (1 - part) * seq_count + (i ^ 1))
        for part in range(2)
        for i in range(seq_count)
    ]
    return lax.ppermute(result[None], ("section", "seq"), across)


def solution(mesh):
    placed = (
        P("section", "seq", "grp"),
        P("section", "seq", "grp"),
        P("section", "seq", "grp"),
        P("section", "seq", "grp"),
        P("section", None, "grp", None),
        P("section"),
        P("section", "grp", None),
        P("section", "grp"),
        P(),
        P(),
    )
    return jax.shard_map(
        body, mesh=mesh, in_specs=placed, out_specs=P("section", "seq", "grp"), check_vma=False
    )
```

```python
import math

import jax
import jax.numpy as jnp
from jax import lax
from jax.experimental import pallas as pl
from jax.experimental.pallas import tpu as pltpu
from jax.sharding import PartitionSpec as P

HD = 128
TILE = 128
BLOCK = 256
PAIR = 2 * BLOCK
CHIPS = 4
FAR = -30000.0
EXP2_SCALE = HD ** (-0.5) * math.log2(math.e)
PIECES = 5
TEXT_LANE = 4 * PIECES
ODD_LANE, CORE_LANE = 32, 33
BF16 = jnp.bfloat16
F32 = jnp.float32
SMEM = pl.BlockSpec(memory_space=pltpu.SMEM)
VMEM = pl.BlockSpec(memory_space=pltpu.VMEM)
HBM = pl.BlockSpec(memory_space=pltpu.HBM)


def params(mib=16):
    return pltpu.CompilerParams(vmem_limit_bytes=mib * 1024 * 1024)


def normed(block):
    wide = block.astype(F32)
    return (wide * lax.rsqrt(jnp.mean(wide * wide, axis=-1, keepdims=True) + 1e-06)).astype(BF16)


def start_out(
    pair, odd, core, order_ref, band_ref, q_ref, k_ref, v_ref, w_ref, t_ref,
    spread_ref, near_ref, cross_ref, pair_out_ref, mine_ref, mask_ref,
    q_in, k_in, v_in, t_in, stage, order, band, sems, out_sems,
):
    odd, core = odd[0], core[0]
    depth, slots = w_ref.shape[1], t_ref.shape[2]
    width = w_ref.shape[2] // CHIPS
    loads = [
        (k_ref.at[0], k_in),
        (v_ref.at[0], v_in),
        (q_ref.at[0], q_in),
        (t_ref.at[0], t_in),
        (order_ref, order),
        (band_ref, band),
    ]
    loads += [
        (w_ref.at[0, :, pl.ds(target * width, width)], stage.at[target, pl.ds(0, depth)])
        for target in range(CHIPS)
    ]
    loads = [
        pltpu.make_async_copy(source, target, sems.at[i])
        for i, (source, target) in enumerate(loads)
    ]
    for load in loads:
        load.start()

    def halves(load, ref, prepare):
        load.wait()
        a, b = prepare(ref[:, :HD]), prepare(ref[:, HD:])
        return jnp.where(odd == 0, a, b), jnp.where(odd == 0, b, a)

    near_ref[0], key_other = halves(loads[0], k_in, normed)
    near_ref[1], value_other = halves(loads[1], v_in, lambda x: x)
    mine_ref[...], query_other = halves(loads[2], q_in, normed)
    cross_ref[0] = key_other
    cross_ref[1] = value_other
    for at, block in enumerate((key_other, value_other, query_other)):
        pair_out_ref[:, at * HD : (at + 1) * HD] = block
    loads[3].wait()
    for target in range(CHIPS):
        panels = []
        for kind in range(2):
            one, two = (
                jnp.where(odd == 0, t_in[kind, :, at : at + HD], t_in[kind, :, at + HD : at + 2 * HD])
                for at in (4 * target * HD, (4 * target + 2) * HD)
            )
            panels.append((jnp.where(core == 0, one, two), jnp.where(core == 0, two, one)))
        for at, panel in enumerate((panels[0][0], panels[1][0], panels[0][1], panels[1][1])):
            stage[target, depth:, at * HD : (at + 1) * HD] = panel
        stage[target, depth:, 4 * HD :] = jnp.zeros((slots, width - 4 * HD), BF16)
    sent = []
    for target, load in enumerate(loads[6:]):
        load.wait()
        sent.append(
            pltpu.make_async_copy(stage.at[target], spread_ref.at[target], out_sems.at[target])
        )
        sent[-1].start()
    for load in loads[4:6]:
        load.wait()
    mask_ref[...] = mask_rows(pair[0], odd, core, order, band)
    for copy in sent:
        copy.wait()


def mask_rows(own, odd, core, order, band):
    total = order.shape[0] // 4

    def tile_at(pair, slot):
        return order[pair * 4 + ((slot // 2) ^ odd) * 2 + slot % 2]

    lane = lax.broadcasted_iota(jnp.int32, (8, HD), 1)
    row = lax.broadcasted_iota(jnp.int32, (8, HD), 0)
    low = jnp.zeros((8, HD), jnp.int32)
    high = jnp.zeros((8, HD), jnp.int32)
    for slot in range(4):
        tile = tile_at(own, slot)
        low = jnp.where(row == slot, band[0, tile], low)
        high = jnp.where(row == slot, band[1, tile], high)
    held = jnp.full((8, HD), -1, jnp.int32)
    beside = own - 1 + 2 * lax.rem(own, 2)
    for piece, pair in enumerate((own, own ^ 1, own - 2, own + 2, beside)):
        inside = (pair >= 0) & (pair < total)
        kept = jnp.clip(pair, 0, total - 1)
        for slot in range(4):
            tile = jnp.where(inside, tile_at(kept, slot), -1)
            held = jnp.where(lane == 4 * piece + slot, tile, held)
    seen = (held >= low) & (held <= high)
    result = jnp.where((lane <= TEXT_LANE) & jnp.logical_not(seen), F32(FAR), F32(0.0))
    for at, value in ((ODD_LANE, odd), (CORE_LANE, core)):
        result = jnp.where(lane == at, value.astype(F32), result)
    return result


def masked_query(mask_ref, mine_ref, pair_ref):
    query = jnp.concatenate([mine_ref[...], pair_ref[:, 2 * HD :]], axis=0)
    lane = lax.broadcasted_iota(jnp.int32, (TILE, HD), 1)
    lanes = [
        jnp.where(lane <= TEXT_LANE, mask_ref[slot : slot + 1, :], F32(0.0)).astype(BF16)
        for slot in range(4)
    ]
    return jnp.concatenate([query, jnp.concatenate(lanes, axis=0)], axis=1)


def add_keys(total, query, key, key_lanes, value):
    scores = lax.dot_general(
        query,
        jnp.concatenate([key, key_lanes], axis=1),
        (((1,), (1,)), ((), ())),
        preferred_element_type=F32,
    )
    weights = jnp.exp2(scores * EXP2_SCALE).astype(BF16)
    wide = jnp.concatenate([value, jnp.ones_like(value)], axis=1)
    part = lax.dot_general(weights, wide, (((1,), (0,)), ((), ())), preferred_element_type=F32)
    return part if total is None else total + part


def piece_arrays(index, low_ref, high_ref):
    shape = (PAIR, HD)
    row = lax.broadcasted_iota(jnp.int32, shape, 0)
    lane = lax.broadcasted_iota(jnp.int32, shape, 1)
    lanes = jnp.where(lane == 4 * index + row // TILE, F32(1.0), F32(0.0)).astype(BF16)
    key = jnp.concatenate([low_ref[0], high_ref[0]], axis=0)
    value = jnp.concatenate([low_ref[1], high_ref[1]], axis=0)
    return key, lanes, value


def text_arrays(count, mask_ref, text_ref, other_core):
    text = text_ref[...]
    chips, held, _ = text.shape
    key = normed(text[:, :, :HD].reshape(chips * held, HD))
    value = text[:, :, HD:].reshape(chips * held, HD)
    row = lax.broadcasted_iota(jnp.int32, key.shape, 0)
    lane = lax.broadcasted_iota(jnp.int32, key.shape, 1)
    core = mask_ref[0:1, CORE_LANE : CORE_LANE + 1]
    side = 1.0 - core if other_core else core
    slot = (2 * (row // held) * held + row % held).astype(F32) + side * held
    dead = (lane == TEXT_LANE) & (slot >= count[0].astype(F32))
    return key, jnp.where(dead, F32(1.0), F32(0.0)).astype(BF16), value


def first_keys(
    mask_ref, mine_ref, pair_ref, own_ref, other_ref, below_ref, above_ref, total_ref
):
    query = masked_query(mask_ref, mine_ref, pair_ref)
    total = None
    for piece, ref in enumerate((own_ref, other_ref, below_ref, above_ref)):
        total = add_keys(total, query, *piece_arrays(piece, ref.at[0], ref.at[1]))
    total_ref[...] = total


def last_keys(
    count, mask_ref, mine_ref, pair_ref, sum_ref, own_text, core_text, beside_ref, out_ref
):
    query = masked_query(mask_ref, mine_ref, pair_ref)
    texts = zip(
        text_arrays(count, mask_ref, own_text, False), text_arrays(count, mask_ref, core_text, True)
    )
    total = add_keys(sum_ref[...], query, *(jnp.concatenate(both, axis=0) for both in texts))
    pieces = piece_arrays(PIECES - 1, beside_ref.at[0], beside_ref.at[1])
    total = add_keys(total, query, *pieces)
    result = total[:, :HD] / total[:, HD:]
    odd = mask_ref[0:1, ODD_LANE : ODD_LANE + 1] > 0.5
    own, other = result[:BLOCK], result[BLOCK:]
    to_even = jnp.where(odd, other, own).astype(BF16)
    to_odd = jnp.where(odd, own, other).astype(BF16)
    for chip in range(CHIPS):
        out_ref[chip] = to_even
        out_ref[CHIPS + chip] = to_odd


def join(low_ref, high_ref, out_ref):
    out_ref[0] = low_ref[...]
    out_ref[1] = high_ref[...]


def join_pair(low_ref, pair_ref, out_ref):
    out_ref[0] = low_ref[...]
    for kind in range(2):
        out_ref[1, kind] = pair_ref[:, kind * HD : (kind + 1) * HD]


def project(core, heads_ref, weight_ref, rows_ref, gate_ref, kept_ref, sent_ref):
    total = None
    depth, width = 2 * HD, kept_ref.shape[1]
    for chip in range(CHIPS):
        heads = jnp.concatenate([heads_ref[chip], heads_ref[CHIPS + chip]], axis=1)
        part = jnp.dot(heads, weight_ref[chip, :depth], preferred_element_type=F32)
        total = part if total is None else total + part
    low, high = total[:, :width], total[:, width:]
    first = core[0] == 0
    kept = jnp.where(first, low, high)
    kept_ref[...] = rows_ref[...].astype(F32) + gate_ref[...] * kept
    sent_ref[...] = jnp.where(first, high, low).astype(BF16)


def body(rows, queries, keys, values, text_kv, text_count, out_weight, gate, band, tile_order):
    seq_count = lax.axis_size("seq")
    seq = lax.axis_index("seq")
    grp = lax.axis_index("grp")
    place = [at.astype(jnp.int32).reshape(1) for at in (seq >> 1, seq & 1, grp & 1)]
    shape = jax.ShapeDtypeStruct
    width = gate.shape[1]
    depth, slots = out_weight.shape[1], text_kv.shape[2]

    spread_shape = (CHIPS, depth + slots, 2 * width)
    token_shapes = [(2, BLOCK, HD)] * 2 + [(BLOCK, 3 * HD), (BLOCK, HD)]
    loaded = (tile_order, band.T, queries, keys, values, out_weight, text_kv)
    spread, near, cross_out, pair_out, mine, mask = pl.pallas_call(
        start_out,
        out_shape=[shape(spread_shape, BF16)]
        + [pltpu.VMEM(dims, BF16) for dims in token_shapes]
        + [pltpu.VMEM((8, HD), F32)],
        in_specs=[SMEM] * 3 + [HBM] * 7,
        out_specs=[HBM] + [VMEM] * 5,
        scratch_shapes=[pltpu.VMEM((BLOCK, 2 * HD), BF16)] * 3
        + [pltpu.VMEM(dims, BF16) for dims in (text_kv.shape[1:], spread_shape)]
        + [pltpu.SMEM(array.shape, jnp.int32) for array in loaded[:2]]
        + [pltpu.SemaphoreType.DMA((count,)) for count in (6 + CHIPS, CHIPS)],
        compiler_params=params(),
        cost_estimate=pl.CostEstimate(flops=10**6, bytes_accessed=4 * 10**6, transcendentals=0),
    )(*place, *(pltpu.with_memory_space_constraint(a, pltpu.HBM) for a in loaded))

    by_core = [[2 * chip + core for chip in range(CHIPS)] for core in range(2)]
    spread = lax.all_to_all(spread, "grp", 0, 0, axis_index_groups=by_core)

    def swapped(block, mask):
        return lax.ppermute(block, "seq", [(i, i ^ mask) for i in range(seq_count)])

    pair_in = swapped(pair_out, 1)
    far_in = swapped(near, 2)
    cross_in = swapped(cross_out, 3)

    def joined(kernel, low, high):
        return pl.pallas_call(
            kernel,
            out_shape=shape((2, 2, BLOCK, HD), BF16),
            in_specs=[VMEM] * 2,
            compiler_params=params(),
            cost_estimate=pl.CostEstimate(flops=0, bytes_accessed=2**19, transcendentals=0),
        )(low, high)

    own_pair = joined(join_pair, near, pair_in)
    after, _ = lax.optimization_barrier((far_in, own_pair))
    other_pair = joined(join, after, cross_in)
    up = [(i, i + 4) for i in range(seq_count - 4)]
    down = [(i + 4, i) for i in range(seq_count - 4)]
    below = lax.ppermute(own_pair, "seq", up)
    above = lax.ppermute(own_pair, "seq", down)
    mixed = [(i, j) for i, j in up if i % 4 < 2] + [(i, j) for i, j in down if i % 4 >= 2]
    beside = lax.ppermute(other_pair, "seq", mixed)

    own_text = spread[:, depth:, : 2 * HD]
    core_text = lax.ppermute(
        spread[:, depth:, 2 * HD : 4 * HD], "grp", [(g, g ^ 1) for g in range(2 * CHIPS)]
    )

    def cost(pieces):
        size = 4 * PAIR * pieces * PAIR * 256
        return pl.CostEstimate(flops=size, bytes_accessed=10**6, transcendentals=PAIR * pieces * PAIR)

    total = pl.pallas_call(
        first_keys,
        out_shape=shape((PAIR, 2 * HD), F32),
        in_specs=[VMEM] * 7,
        compiler_params=params(),
        cost_estimate=cost(5),
    )(mask, mine, pair_in, own_pair, other_pair, below, above)
    attention = pl.pallas_call(
        last_keys,
        out_shape=shape((2 * CHIPS, BLOCK, HD), BF16),
        in_specs=[SMEM] + [VMEM] * 7,
        compiler_params=params(),
        cost_estimate=cost(1),
    )(text_count, mask, mine, pair_in, total, own_text, core_text, beside)

    groups = [
        [(2 * pair + odd) * 2 * CHIPS + 2 * chip + core for odd in range(2) for chip in range(CHIPS)]
        for pair in range(seq_count // 2)
        for core in range(2)
    ]
    heads = lax.all_to_all(attention, ("seq", "grp"), 0, 0, axis_index_groups=groups)
    kept, sent = pl.pallas_call(
        project,
        out_shape=(shape((BLOCK, width), F32), shape((BLOCK, width), BF16)),
        in_specs=[SMEM] + [VMEM] * 4,
        compiler_params=params(),
        cost_estimate=pl.CostEstimate(
            flops=2 * BLOCK * 1024 * 768, bytes_accessed=3 * 10**6, transcendentals=0
        ),
    )(place[2], heads, spread, rows[0], gate)
    other = lax.ppermute(sent, "grp", [(g, g ^ 1) for g in range(2 * CHIPS)])
    result = (kept + gate * other.astype(F32)).astype(BF16)
    return lax.ppermute(result, "section", [(0, 1), (1, 0)])[None]


def solution(mesh):
    placed = (
        P("section", "seq", "grp"),
        P("section", "seq", "grp"),
        P("section", "seq", "grp"),
        P("section", "seq", "grp"),
        P("section", None, "grp", None),
        P("section"),
        P("section", "grp", None),
        P("section", "grp"),
        P(),
        P(),
    )
    return jax.shard_map(
        body, mesh=mesh, in_specs=placed, out_specs=P("section", "seq", "grp"), check_vma=False
    )
```

```python
import math

import jax
import jax.numpy as jnp
from jax import lax
from jax.experimental import pallas as pl
from jax.experimental.pallas import tpu as pltpu
from jax.sharding import PartitionSpec as P

HD = 128
TILE = 128
BLOCK = 256
PAIR = 2 * BLOCK
CHIPS = 4
FAR = -30000.0
EXP2_SCALE = HD ** (-0.5) * math.log2(math.e)
PIECES = 5
TEXT_LANE = 4 * PIECES
ODD_LANE, CORE_LANE = 32, 33
BF16 = jnp.bfloat16
F32 = jnp.float32
SMEM = pl.BlockSpec(memory_space=pltpu.SMEM)
VMEM = pl.BlockSpec(memory_space=pltpu.VMEM)
HBM = pl.BlockSpec(memory_space=pltpu.HBM)


def params(mib=16):
    return pltpu.CompilerParams(vmem_limit_bytes=mib * 1024 * 1024)


def normed(block):
    wide = block.astype(F32)
    return (wide * lax.rsqrt(jnp.mean(wide * wide, axis=-1, keepdims=True) + 1e-06)).astype(BF16)


def start_out(
    pair, odd, core, order_ref, band_ref, q_ref, k_ref, v_ref, w_ref, t_ref,
    spread_ref, near_ref, cross_ref, pair_out_ref, mine_ref, mask_ref,
    q_in, k_in, v_in, t_in, stage, order, band, sems, out_sems,
):
    odd, core = odd[0], core[0]
    depth, slots = w_ref.shape[1], t_ref.shape[2]
    width = w_ref.shape[2] // CHIPS
    loads = [
        (k_ref.at[0], k_in),
        (v_ref.at[0], v_in),
        (q_ref.at[0], q_in),
        (t_ref.at[0], t_in),
        (order_ref, order),
        (band_ref, band),
    ]
    loads += [
        (w_ref.at[0, :, pl.ds(target * width, width)], stage.at[target, pl.ds(0, depth)])
        for target in range(CHIPS)
    ]
    loads = [
        pltpu.make_async_copy(source, target, sems.at[i])
        for i, (source, target) in enumerate(loads)
    ]
    for load in loads:
        load.start()

    def halves(load, ref, prepare):
        load.wait()
        a, b = prepare(ref[:, :HD]), prepare(ref[:, HD:])
        return jnp.where(odd == 0, a, b), jnp.where(odd == 0, b, a)

    near_ref[0], key_other = halves(loads[0], k_in, normed)
    near_ref[1], value_other = halves(loads[1], v_in, lambda x: x)
    mine_ref[...], query_other = halves(loads[2], q_in, normed)
    cross_ref[0] = key_other
    cross_ref[1] = value_other
    for at, block in enumerate((key_other, value_other, query_other)):
        pair_out_ref[:, at * HD : (at + 1) * HD] = block
    loads[3].wait()
    for target in range(CHIPS):
        panels = []
        for kind in range(2):
            one, two = (
                jnp.where(odd == 0, t_in[kind, :, at : at + HD], t_in[kind, :, at + HD : at + 2 * HD])
                for at in (4 * target * HD, (4 * target + 2) * HD)
            )
            panels.append((jnp.where(core == 0, one, two), jnp.where(core == 0, two, one)))
        for at, panel in enumerate((panels[0][0], panels[1][0], panels[0][1], panels[1][1])):
            stage[target, depth:, at * HD : (at + 1) * HD] = panel
        stage[target, depth:, 4 * HD :] = jnp.zeros((slots, width - 4 * HD), BF16)
    sent = []
    for target, load in enumerate(loads[6:]):
        load.wait()
        sent.append(
            pltpu.make_async_copy(stage.at[target], spread_ref.at[target], out_sems.at[target])
        )
        sent[-1].start()
    for load in loads[4:6]:
        load.wait()
    mask_ref[...] = mask_rows(pair[0], odd, core, order, band)
    for copy in sent:
        copy.wait()


def mask_rows(own, odd, core, order, band):
    total = order.shape[0] // 4

    def tile_at(pair, slot):
        return order[pair * 4 + ((slot // 2) ^ odd) * 2 + slot % 2]

    lane = lax.broadcasted_iota(jnp.int32, (8, HD), 1)
    row = lax.broadcasted_iota(jnp.int32, (8, HD), 0)
    low = jnp.zeros((8, HD), jnp.int32)
    high = jnp.zeros((8, HD), jnp.int32)
    for slot in range(4):
        tile = tile_at(own, slot)
        low = jnp.where(row == slot, band[0, tile], low)
        high = jnp.where(row == slot, band[1, tile], high)
    held = jnp.full((8, HD), -1, jnp.int32)
    beside = own - 1 + 2 * lax.rem(own, 2)
    for piece, pair in enumerate((own, own ^ 1, own - 2, own + 2, beside)):
        inside = (pair >= 0) & (pair < total)
        kept = jnp.clip(pair, 0, total - 1)
        for slot in range(4):
            tile = jnp.where(inside, tile_at(kept, slot), -1)
            held = jnp.where(lane == 4 * piece + slot, tile, held)
    seen = (held >= low) & (held <= high)
    result = jnp.where((lane <= TEXT_LANE) & jnp.logical_not(seen), F32(FAR), F32(0.0))
    for at, value in ((ODD_LANE, odd), (CORE_LANE, core)):
        result = jnp.where(lane == at, value.astype(F32), result)
    return result


def masked_query(mask_ref, mine_ref, pair_ref):
    query = jnp.concatenate([mine_ref[...], pair_ref[:, 2 * HD :]], axis=0)
    lane = lax.broadcasted_iota(jnp.int32, (TILE, HD), 1)
    lanes = [
        jnp.where(lane <= TEXT_LANE, mask_ref[slot : slot + 1, :], F32(0.0)).astype(BF16)
        for slot in range(4)
    ]
    return jnp.concatenate([query, jnp.concatenate(lanes, axis=0)], axis=1)


def add_keys(total, query, key, key_lanes, value):
    scores = lax.dot_general(
        query,
        jnp.concatenate([key, key_lanes], axis=1),
        (((1,), (1,)), ((), ())),
        preferred_element_type=F32,
    )
    weights = jnp.exp2(scores * EXP2_SCALE).astype(BF16)
    wide = jnp.concatenate([value, jnp.ones_like(value)], axis=1)
    part = lax.dot_general(weights, wide, (((1,), (0,)), ((), ())), preferred_element_type=F32)
    return part if total is None else total + part


def piece_arrays(index, low_ref, high_ref):
    shape = (PAIR, HD)
    row = lax.broadcasted_iota(jnp.int32, shape, 0)
    lane = lax.broadcasted_iota(jnp.int32, shape, 1)
    lanes = jnp.where(lane == 4 * index + row // TILE, F32(1.0), F32(0.0)).astype(BF16)
    key = jnp.concatenate([low_ref[0], high_ref[0]], axis=0)
    value = jnp.concatenate([low_ref[1], high_ref[1]], axis=0)
    return key, lanes, value


def text_arrays(count, mask_ref, text_ref, other_core):
    text = text_ref[...]
    chips, held, _ = text.shape
    key = normed(text[:, :, :HD].reshape(chips * held, HD))
    value = text[:, :, HD:].reshape(chips * held, HD)
    row = lax.broadcasted_iota(jnp.int32, key.shape, 0)
    lane = lax.broadcasted_iota(jnp.int32, key.shape, 1)
    core = mask_ref[0:1, CORE_LANE : CORE_LANE + 1]
    side = 1.0 - core if other_core else core
    slot = (2 * (row // held) * held + row % held).astype(F32) + side * held
    dead = (lane == TEXT_LANE) & (slot >= count[0].astype(F32))
    return key, jnp.where(dead, F32(1.0), F32(0.0)).astype(BF16), value


def first_keys(
    mask_ref, mine_ref, pair_ref, own_ref, other_ref, below_ref, above_ref, total_ref
):
    query = masked_query(mask_ref, mine_ref, pair_ref)
    total = None
    for piece, ref in enumerate((own_ref, other_ref, below_ref, above_ref)):
        total = add_keys(total, query, *piece_arrays(piece, ref.at[0], ref.at[1]))
    total_ref[...] = total


def last_keys(
    count, mask_ref, mine_ref, pair_ref, sum_ref, own_text, core_text, beside_ref, out_ref
):
    query = masked_query(mask_ref, mine_ref, pair_ref)
    texts = zip(
        text_arrays(count, mask_ref, own_text, False), text_arrays(count, mask_ref, core_text, True)
    )
    total = add_keys(sum_ref[...], query, *(jnp.concatenate(both, axis=0) for both in texts))
    pieces = piece_arrays(PIECES - 1, beside_ref.at[0], beside_ref.at[1])
    total = add_keys(total, query, *pieces)
    result = total[:, :HD] / total[:, HD:]
    odd = mask_ref[0:1, ODD_LANE : ODD_LANE + 1] > 0.5
    own, other = result[:BLOCK], result[BLOCK:]
    to_even = jnp.where(odd, other, own).astype(BF16)
    to_odd = jnp.where(odd, own, other).astype(BF16)
    for chip in range(CHIPS):
        out_ref[chip] = to_even
        out_ref[CHIPS + chip] = to_odd


def join(low_ref, high_ref, out_ref):
    out_ref[0] = low_ref[...]
    out_ref[1] = high_ref[...]


def join_pair(low_ref, pair_ref, out_ref):
    out_ref[0] = low_ref[...]
    for kind in range(2):
        out_ref[1, kind] = pair_ref[:, kind * HD : (kind + 1) * HD]


def projected(core, heads_ref, weight_ref, width):
    total = None
    columns = pl.ds(pl.multiple_of(core * width, 128), width)
    for chip in range(CHIPS):
        heads = jnp.concatenate([heads_ref[chip], heads_ref[CHIPS + chip]], axis=1)
        weight = weight_ref[chip, : 2 * HD, columns]
        part = jnp.dot(heads, weight, preferred_element_type=F32)
        total = part if total is None else total + part
    return total


def project_other(core, heads_ref, weight_ref, out_ref):
    out_ref[...] = projected(1 - core[0], heads_ref, weight_ref, out_ref.shape[1]).astype(BF16)


def project_own(core, heads_ref, weight_ref, rows_ref, gate_ref, out_ref):
    share = projected(core[0], heads_ref, weight_ref, out_ref.shape[1])
    out_ref[...] = rows_ref[...].astype(F32) + gate_ref[...] * share


def body(rows, queries, keys, values, text_kv, text_count, out_weight, gate, band, tile_order):
    seq_count = lax.axis_size("seq")
    seq = lax.axis_index("seq")
    grp = lax.axis_index("grp")
    place = [at.astype(jnp.int32).reshape(1) for at in (seq >> 1, seq & 1, grp & 1)]
    shape = jax.ShapeDtypeStruct
    width = gate.shape[1]
    depth, slots = out_weight.shape[1], text_kv.shape[2]

    spread_shape = (CHIPS, depth + slots, 2 * width)
    token_shapes = [(2, BLOCK, HD)] * 2 + [(BLOCK, 3 * HD), (BLOCK, HD)]
    loaded = (tile_order, band.T, queries, keys, values, out_weight, text_kv)
    spread, near, cross_out, pair_out, mine, mask = pl.pallas_call(
        start_out,
        out_shape=[shape(spread_shape, BF16)]
        + [pltpu.VMEM(dims, BF16) for dims in token_shapes]
        + [pltpu.VMEM((8, HD), F32)],
        in_specs=[SMEM] * 3 + [HBM] * 7,
        out_specs=[HBM] + [VMEM] * 5,
        scratch_shapes=[pltpu.VMEM((BLOCK, 2 * HD), BF16)] * 3
        + [pltpu.VMEM(dims, BF16) for dims in (text_kv.shape[1:], spread_shape)]
        + [pltpu.SMEM(array.shape, jnp.int32) for array in loaded[:2]]
        + [pltpu.SemaphoreType.DMA((count,)) for count in (6 + CHIPS, CHIPS)],
        compiler_params=params(),
        cost_estimate=pl.CostEstimate(flops=10**6, bytes_accessed=4 * 10**6, transcendentals=0),
    )(*place, *(pltpu.with_memory_space_constraint(a, pltpu.HBM) for a in loaded))

    by_core = [[2 * chip + core for chip in range(CHIPS)] for core in range(2)]
    spread = lax.all_to_all(spread, "grp", 0, 0, axis_index_groups=by_core)

    def swapped(block, mask):
        return lax.ppermute(block, "seq", [(i, i ^ mask) for i in range(seq_count)])

    pair_in = swapped(pair_out, 1)
    far_in = swapped(near, 2)
    cross_in = swapped(cross_out, 3)

    def joined(kernel, low, high):
        return pl.pallas_call(
            kernel,
            out_shape=shape((2, 2, BLOCK, HD), BF16),
            in_specs=[VMEM] * 2,
            compiler_params=params(),
            cost_estimate=pl.CostEstimate(flops=0, bytes_accessed=2**19, transcendentals=0),
        )(low, high)

    own_pair = joined(join_pair, near, pair_in)
    after, _ = lax.optimization_barrier((far_in, own_pair))
    other_pair = joined(join, after, cross_in)
    up = [(i, i + 4) for i in range(seq_count - 4)]
    down = [(i + 4, i) for i in range(seq_count - 4)]
    below = lax.ppermute(own_pair, "seq", up)
    above = lax.ppermute(own_pair, "seq", down)
    mixed = [(i, j) for i, j in up if i % 4 < 2] + [(i, j) for i, j in down if i % 4 >= 2]
    beside = lax.ppermute(other_pair, "seq", mixed)

    own_text = spread[:, depth:, : 2 * HD]
    core_text = lax.ppermute(
        spread[:, depth:, 2 * HD : 4 * HD], "grp", [(g, g ^ 1) for g in range(2 * CHIPS)]
    )

    def cost(pieces):
        size = 4 * PAIR * pieces * PAIR * 256
        return pl.CostEstimate(flops=size, bytes_accessed=10**6, transcendentals=PAIR * pieces * PAIR)

    total = pl.pallas_call(
        first_keys,
        out_shape=shape((PAIR, 2 * HD), F32),
        in_specs=[VMEM] * 7,
        compiler_params=params(),
        cost_estimate=cost(5),
    )(mask, mine, pair_in, own_pair, other_pair, below, above)
    attention = pl.pallas_call(
        last_keys,
        out_shape=shape((2 * CHIPS, BLOCK, HD), BF16),
        in_specs=[SMEM] + [VMEM] * 7,
        compiler_params=params(),
        cost_estimate=cost(1),
    )(text_count, mask, mine, pair_in, total, own_text, core_text, beside)

    groups = [
        [(2 * pair + odd) * 2 * CHIPS + 2 * chip + core for odd in range(2) for chip in range(CHIPS)]
        for pair in range(seq_count // 2)
        for core in range(2)
    ]
    heads = lax.all_to_all(attention, ("seq", "grp"), 0, 0, axis_index_groups=groups)
    half = pl.CostEstimate(flops=2 * BLOCK * 1024 * 384, bytes_accessed=10**6, transcendentals=0)
    sent = pl.pallas_call(
        project_other,
        out_shape=shape((BLOCK, width), BF16),
        in_specs=[SMEM] + [VMEM] * 2,
        compiler_params=params(),
        cost_estimate=half,
    )(place[2], heads, spread)
    kept = pl.pallas_call(
        project_own,
        out_shape=shape((BLOCK, width), F32),
        in_specs=[SMEM] + [VMEM] * 4,
        compiler_params=params(),
        cost_estimate=half,
    )(place[2], heads, spread, rows[0], gate)
    other = lax.ppermute(sent, "grp", [(g, g ^ 1) for g in range(2 * CHIPS)])
    result = (kept + gate * other.astype(F32)).astype(BF16)
    return lax.ppermute(result, "section", [(0, 1), (1, 0)])[None]


def solution(mesh):
    placed = (
        P("section", "seq", "grp"),
        P("section", "seq", "grp"),
        P("section", "seq", "grp"),
        P("section", "seq", "grp"),
        P("section", None, "grp", None),
        P("section"),
        P("section", "grp", None),
        P("section", "grp"),
        P(),
        P(),
    )
    return jax.shard_map(
        body, mesh=mesh, in_specs=placed, out_specs=P("section", "seq", "grp"), check_vma=False
    )
```

```python
import math

import jax
import jax.numpy as jnp
from jax import lax
from jax.experimental import pallas as pl
from jax.experimental.pallas import tpu as pltpu
from jax.sharding import PartitionSpec as P

HD = 128
TILE = 128
BLOCK = 256
PAIR = 2 * BLOCK
CHIPS = 4
FAR = -30000.0
EXP2_SCALE = HD ** (-0.5) * math.log2(math.e)
PIECES = 5
TEXT_LANE = 4 * PIECES
ODD_LANE, CORE_LANE = 32, 33
BF16 = jnp.bfloat16
F32 = jnp.float32
SMEM = pl.BlockSpec(memory_space=pltpu.SMEM)
VMEM = pl.BlockSpec(memory_space=pltpu.VMEM)
HBM = pl.BlockSpec(memory_space=pltpu.HBM)


def params(mib=16):
    return pltpu.CompilerParams(vmem_limit_bytes=mib * 1024 * 1024)


def normed(block):
    wide = block.astype(F32)
    return (wide * lax.rsqrt(jnp.mean(wide * wide, axis=-1, keepdims=True) + 1e-06)).astype(BF16)


def start_out(
    pair, odd, core, order_ref, band_ref, q_ref, k_ref, v_ref, w_ref, t_ref,
    spread_ref, near_ref, cross_ref, pair_out_ref, mine_ref, mask_ref,
    q_in, k_in, v_in, t_in, stage, order, band, sems, out_sems,
):
    odd, core = odd[0], core[0]
    depth, slots = w_ref.shape[1], t_ref.shape[2]
    width = w_ref.shape[2] // CHIPS
    loads = [
        (k_ref.at[0], k_in),
        (v_ref.at[0], v_in),
        (q_ref.at[0], q_in),
        (t_ref.at[0], t_in),
        (order_ref, order),
        (band_ref, band),
    ]
    loads += [
        (w_ref.at[0, :, pl.ds(target * width, width)], stage.at[target, pl.ds(0, depth)])
        for target in range(CHIPS)
    ]
    loads = [
        pltpu.make_async_copy(source, target, sems.at[i])
        for i, (source, target) in enumerate(loads)
    ]
    for load in loads:
        load.start()

    def halves(load, ref, prepare):
        load.wait()
        a, b = prepare(ref[:, :HD]), prepare(ref[:, HD:])
        return jnp.where(odd == 0, a, b), jnp.where(odd == 0, b, a)

    near_ref[0], key_other = halves(loads[0], k_in, normed)
    near_ref[1], value_other = halves(loads[1], v_in, lambda x: x)
    mine_ref[...], query_other = halves(loads[2], q_in, normed)
    cross_ref[0] = key_other
    cross_ref[1] = value_other
    for at, block in enumerate((key_other, value_other, query_other)):
        pair_out_ref[:, at * HD : (at + 1) * HD] = block
    loads[3].wait()
    for target in range(CHIPS):
        panels = []
        for kind in range(2):
            one, two = (
                jnp.where(odd == 0, t_in[kind, :, at : at + HD], t_in[kind, :, at + HD : at + 2 * HD])
                for at in (4 * target * HD, (4 * target + 2) * HD)
            )
            panels.append((jnp.where(core == 0, one, two), jnp.where(core == 0, two, one)))
        for at, panel in enumerate((panels[0][0], panels[1][0], panels[0][1], panels[1][1])):
            stage[target, depth:, at * HD : (at + 1) * HD] = panel
        stage[target, depth:, 4 * HD :] = jnp.zeros((slots, width - 4 * HD), BF16)
    sent = []
    for target, load in enumerate(loads[6:]):
        load.wait()
        sent.append(
            pltpu.make_async_copy(stage.at[target], spread_ref.at[target], out_sems.at[target])
        )
        sent[-1].start()
    for load in loads[4:6]:
        load.wait()
    mask_ref[...] = mask_rows(pair[0], odd, core, order, band)
    for copy in sent:
        copy.wait()


def mask_rows(own, odd, core, order, band):
    total = order.shape[0] // 4

    def tile_at(pair, slot):
        return order[pair * 4 + ((slot // 2) ^ odd) * 2 + slot % 2]

    lane = lax.broadcasted_iota(jnp.int32, (8, HD), 1)
    row = lax.broadcasted_iota(jnp.int32, (8, HD), 0)
    low = jnp.zeros((8, HD), jnp.int32)
    high = jnp.zeros((8, HD), jnp.int32)
    for slot in range(4):
        tile = tile_at(own, slot)
        low = jnp.where(row == slot, band[0, tile], low)
        high = jnp.where(row == slot, band[1, tile], high)
    held = jnp.full((8, HD), -1, jnp.int32)
    beside = own - 1 + 2 * lax.rem(own, 2)
    for piece, pair in enumerate((own, own ^ 1, own - 2, own + 2, beside)):
        inside = (pair >= 0) & (pair < total)
        kept = jnp.clip(pair, 0, total - 1)
        for slot in range(4):
            tile = jnp.where(inside, tile_at(kept, slot), -1)
            held = jnp.where(lane == 4 * piece + slot, tile, held)
    seen = (held >= low) & (held <= high)
    result = jnp.where((lane <= TEXT_LANE) & jnp.logical_not(seen), F32(FAR), F32(0.0))
    for at, value in ((ODD_LANE, odd), (CORE_LANE, core)):
        result = jnp.where(lane == at, value.astype(F32), result)
    return result


def masked_query(mask_ref, mine_ref, pair_ref):
    query = jnp.concatenate([mine_ref[...], pair_ref[:, 2 * HD :]], axis=0)
    lane = lax.broadcasted_iota(jnp.int32, (TILE, HD), 1)
    lanes = [
        jnp.where(lane <= TEXT_LANE, mask_ref[slot : slot + 1, :], F32(0.0)).astype(BF16)
        for slot in range(4)
    ]
    return jnp.concatenate([query, jnp.concatenate(lanes, axis=0)], axis=1)


def add_keys(total, query, key, key_lanes, value):
    scores = lax.dot_general(
        query,
        jnp.concatenate([key, key_lanes], axis=1),
        (((1,), (1,)), ((), ())),
        preferred_element_type=F32,
    )
    weights = jnp.exp2(scores * EXP2_SCALE).astype(BF16)
    wide = jnp.concatenate([value, jnp.ones_like(value)], axis=1)
    part = lax.dot_general(weights, wide, (((1,), (0,)), ((), ())), preferred_element_type=F32)
    return part if total is None else total + part


def piece_arrays(index, low_ref, high_ref):
    shape = (PAIR, HD)
    row = lax.broadcasted_iota(jnp.int32, shape, 0)
    lane = lax.broadcasted_iota(jnp.int32, shape, 1)
    lanes = jnp.where(lane == 4 * index + row // TILE, F32(1.0), F32(0.0)).astype(BF16)
    key = jnp.concatenate([low_ref[0], high_ref[0]], axis=0)
    value = jnp.concatenate([low_ref[1], high_ref[1]], axis=0)
    return key, lanes, value


def text_arrays(count, mask_ref, text_ref, other_core):
    text = text_ref[...]
    chips, held, _ = text.shape
    key = normed(text[:, :, :HD].reshape(chips * held, HD))
    value = text[:, :, HD:].reshape(chips * held, HD)
    row = lax.broadcasted_iota(jnp.int32, key.shape, 0)
    lane = lax.broadcasted_iota(jnp.int32, key.shape, 1)
    core = mask_ref[0:1, CORE_LANE : CORE_LANE + 1]
    side = 1.0 - core if other_core else core
    slot = (2 * (row // held) * held + row % held).astype(F32) + side * held
    dead = (lane == TEXT_LANE) & (slot >= count[0].astype(F32))
    return key, jnp.where(dead, F32(1.0), F32(0.0)).astype(BF16), value


def first_keys(
    mask_ref, mine_ref, pair_ref, own_ref, other_ref, below_ref, above_ref, total_ref
):
    query = masked_query(mask_ref, mine_ref, pair_ref)
    total = None
    for piece, ref in enumerate((own_ref, other_ref, below_ref, above_ref)):
        total = add_keys(total, query, *piece_arrays(piece, ref.at[0], ref.at[1]))
    total_ref[...] = total


def last_keys(
    count, mask_ref, mine_ref, pair_ref, sum_ref, own_text, core_text, beside_ref, out_ref
):
    query = masked_query(mask_ref, mine_ref, pair_ref)
    texts = [
        text_arrays(count, mask_ref, own_text, False),
        text_arrays(count, mask_ref, core_text, True),
    ]
    pieces = piece_arrays(PIECES - 1, beside_ref.at[0], beside_ref.at[1])
    together = (jnp.concatenate(three, axis=0) for three in zip(*texts, pieces))
    total = add_keys(sum_ref[...], query, *together)
    result = total[:, :HD] / total[:, HD:]
    odd = mask_ref[0:1, ODD_LANE : ODD_LANE + 1] > 0.5
    own, other = result[:BLOCK], result[BLOCK:]
    to_even = jnp.where(odd, other, own).astype(BF16)
    to_odd = jnp.where(odd, own, other).astype(BF16)
    for chip in range(CHIPS):
        out_ref[chip] = to_even
        out_ref[CHIPS + chip] = to_odd


def join(low_ref, high_ref, out_ref):
    out_ref[0] = low_ref[...]
    out_ref[1] = high_ref[...]


def join_pair(low_ref, pair_ref, out_ref):
    out_ref[0] = low_ref[...]
    for kind in range(2):
        out_ref[1, kind] = pair_ref[:, kind * HD : (kind + 1) * HD]


def projected(core, heads_ref, weight_ref, width):
    total = None
    columns = pl.ds(pl.multiple_of(core * width, 128), width)
    for chip in range(CHIPS):
        heads = jnp.concatenate([heads_ref[chip], heads_ref[CHIPS + chip]], axis=1)
        weight = weight_ref[chip, : 2 * HD, columns]
        part = jnp.dot(heads, weight, preferred_element_type=F32)
        total = part if total is None else total + part
    return total


def project_other(core, heads_ref, weight_ref, out_ref):
    out_ref[...] = projected(1 - core[0], heads_ref, weight_ref, out_ref.shape[1]).astype(BF16)


def project_own(core, heads_ref, weight_ref, rows_ref, gate_ref, out_ref):
    share = projected(core[0], heads_ref, weight_ref, out_ref.shape[1])
    out_ref[...] = rows_ref[...].astype(F32) + gate_ref[...] * share


def body(rows, queries, keys, values, text_kv, text_count, out_weight, gate, band, tile_order):
    seq_count = lax.axis_size("seq")
    seq = lax.axis_index("seq")
    grp = lax.axis_index("grp")
    place = [at.astype(jnp.int32).reshape(1) for at in (seq >> 1, seq & 1, grp & 1)]
    shape = jax.ShapeDtypeStruct
    width = gate.shape[1]
    depth, slots = out_weight.shape[1], text_kv.shape[2]

    spread_shape = (CHIPS, depth + slots, 2 * width)
    token_shapes = [(2, BLOCK, HD)] * 2 + [(BLOCK, 3 * HD), (BLOCK, HD)]
    loaded = (tile_order, band.T, queries, keys, values, out_weight, text_kv)
    spread, near, cross_out, pair_out, mine, mask = pl.pallas_call(
        start_out,
        out_shape=[shape(spread_shape, BF16)]
        + [pltpu.VMEM(dims, BF16) for dims in token_shapes]
        + [pltpu.VMEM((8, HD), F32)],
        in_specs=[SMEM] * 3 + [HBM] * 7,
        out_specs=[HBM] + [VMEM] * 5,
        scratch_shapes=[pltpu.VMEM((BLOCK, 2 * HD), BF16)] * 3
        + [pltpu.VMEM(dims, BF16) for dims in (text_kv.shape[1:], spread_shape)]
        + [pltpu.SMEM(array.shape, jnp.int32) for array in loaded[:2]]
        + [pltpu.SemaphoreType.DMA((count,)) for count in (6 + CHIPS, CHIPS)],
        compiler_params=params(),
        cost_estimate=pl.CostEstimate(flops=10**6, bytes_accessed=4 * 10**6, transcendentals=0),
    )(*place, *(pltpu.with_memory_space_constraint(a, pltpu.HBM) for a in loaded))

    by_core = [[2 * chip + core for chip in range(CHIPS)] for core in range(2)]
    spread = lax.all_to_all(spread, "grp", 0, 0, axis_index_groups=by_core)

    def swapped(block, mask):
        return lax.ppermute(block, "seq", [(i, i ^ mask) for i in range(seq_count)])

    pair_in = swapped(pair_out, 1)
    far_in = swapped(near, 2)
    cross_in = swapped(cross_out, 3)

    def joined(kernel, low, high):
        return pl.pallas_call(
            kernel,
            out_shape=shape((2, 2, BLOCK, HD), BF16),
            in_specs=[VMEM] * 2,
            compiler_params=params(),
            cost_estimate=pl.CostEstimate(flops=0, bytes_accessed=2**19, transcendentals=0),
        )(low, high)

    own_pair = joined(join_pair, near, pair_in)
    after, _ = lax.optimization_barrier((far_in, own_pair))
    other_pair = joined(join, after, cross_in)
    up = [(i, i + 4) for i in range(seq_count - 4)]
    down = [(i + 4, i) for i in range(seq_count - 4)]
    below = lax.ppermute(own_pair, "seq", up)
    above = lax.ppermute(own_pair, "seq", down)
    mixed = [(i, j) for i, j in up if i % 4 < 2] + [(i, j) for i, j in down if i % 4 >= 2]
    beside = lax.ppermute(other_pair, "seq", mixed)

    own_text = spread[:, depth:, : 2 * HD]
    core_text = lax.ppermute(
        spread[:, depth:, 2 * HD : 4 * HD], "grp", [(g, g ^ 1) for g in range(2 * CHIPS)]
    )

    def cost(pieces):
        size = 4 * PAIR * pieces * PAIR * 256
        return pl.CostEstimate(flops=size, bytes_accessed=10**6, transcendentals=PAIR * pieces * PAIR)

    total = pl.pallas_call(
        first_keys,
        out_shape=shape((PAIR, 2 * HD), F32),
        in_specs=[VMEM] * 7,
        compiler_params=params(),
        cost_estimate=cost(5),
    )(mask, mine, pair_in, own_pair, other_pair, below, above)
    attention = pl.pallas_call(
        last_keys,
        out_shape=shape((2 * CHIPS, BLOCK, HD), BF16),
        in_specs=[SMEM] + [VMEM] * 7,
        compiler_params=params(),
        cost_estimate=cost(1),
    )(text_count, mask, mine, pair_in, total, own_text, core_text, beside)

    groups = [
        [(2 * pair + odd) * 2 * CHIPS + 2 * chip + core for odd in range(2) for chip in range(CHIPS)]
        for pair in range(seq_count // 2)
        for core in range(2)
    ]
    heads = lax.all_to_all(attention, ("seq", "grp"), 0, 0, axis_index_groups=groups)
    half = pl.CostEstimate(flops=2 * BLOCK * 1024 * 384, bytes_accessed=10**6, transcendentals=0)
    sent = pl.pallas_call(
        project_other,
        out_shape=shape((BLOCK, width), BF16),
        in_specs=[SMEM] + [VMEM] * 2,
        compiler_params=params(),
        cost_estimate=half,
    )(place[2], heads, spread)
    kept = pl.pallas_call(
        project_own,
        out_shape=shape((BLOCK, width), F32),
        in_specs=[SMEM] + [VMEM] * 4,
        compiler_params=params(),
        cost_estimate=half,
    )(place[2], heads, spread, rows[0], gate)
    other = lax.ppermute(sent, "grp", [(g, g ^ 1) for g in range(2 * CHIPS)])
    result = (kept + gate * other.astype(F32)).astype(BF16)
    return lax.ppermute(result, "section", [(0, 1), (1, 0)])[None]


def solution(mesh):
    placed = (
        P("section", "seq", "grp"),
        P("section", "seq", "grp"),
        P("section", "seq", "grp"),
        P("section", "seq", "grp"),
        P("section", None, "grp", None),
        P("section"),
        P("section", "grp", None),
        P("section", "grp"),
        P(),
        P(),
    )
    return jax.shard_map(
        body, mesh=mesh, in_specs=placed, out_specs=P("section", "seq", "grp"), check_vma=False
    )
```
